32 devices in a mesh: dp: 16 (over z, y, x), tensor: 2 (over core).
Axes of the slice: x: 2, y: 2, z: 4, core: 2. Of those that a mesh axis runs over, the one named last changes fastest.
Arguments:
- tokens: bfloat16 [32768, 1024], P(('dp', 'tensor')), may hold values from -6 to 6
- norm_gain1: float32 [1024], replicated, may hold values from 0.1 to 1.9
- in_weight: bfloat16 [1024, 3, 1024], P('dp', None, 'tensor'), may hold values from -0.1875 to 0.1875
- conv_kernel: bfloat16 [3, 1024], P(None, 'tensor'), may hold values from -3.5 to 3.5
- out_weight: bfloat16 [1024, 1024], P('dp', 'tensor'), may hold values from -0.1875 to 0.1875
- norm_gain2: float32 [1024], replicated, may hold values from 0.1 to 1.9
- gate_up_weight: bfloat16 [1024, 2, 4608], P('dp', None, 'tensor'), may hold values from -0.1875 to 0.1875
- down_weight: bfloat16 [1024, 4608], P('dp', 'tensor'), may hold values from -0.09375 to 0.09375
- out_grad: bfloat16 [32768, 1024], P(('dp', 'tensor')), may hold values from -6 to 6
Outputs:
- mixed_out: bfloat16 [32768, 1024], P(('dp', 'tensor'))
- input_grad: float32 [32768, 1024], P(('dp', 'tensor'))
- gain1_grad: float32 [1024], replicated
- in_weight_grad: float32 [1024, 3, 1024], P('dp', None, 'tensor')
- conv_grad: float32 [3, 1024], P(None, 'tensor')
- out_weight_grad: float32 [1024, 1024], P('dp', 'tensor')
- gain2_grad: float32 [1024], replicated
- gate_up_grad: float32 [1024, 2, 4608], P('dp', None, 'tensor')
- down_grad: float32 [1024, 4608], P('dp', 'tensor')
The draws below stay inside these ranges and needn't reach their ends.
All inputs are finite; a program needn't handle non-finite values.
Results may differ from the reference program's by a relative error of at most 0.011.
Values may be sent and summed in bfloat16 or wider, within the bound.
No kernel may reach another device: no remote copies, remote signals or barrier semaphores. Data moves between devices by JAX's collectives and lax.ppermute only.
A program may use at most 320 MiB of HBM per device.

```python
import jax
import jax.numpy as jnp
from jax import lax

D = 1024
FF = 4608
LEN = 1024
TOK_DEV = 1024
TOKENS = 32768
N_TENSOR = 2


def level_of(own_key, extent, shards, low, high):
    def one(dim, blocks):
        draws = jax.random.uniform(jax.random.fold_in(jax.random.fold_in(own_key, 6), dim), (blocks,), jnp.float32, low / len(shards), high / len(shards))
        return jnp.repeat(jnp.exp(draws), extent[dim] // blocks).reshape((-1,) + (1,) * (len(extent) - dim - 1))

    gain = one(*shards[0])
    for cut in shards[1:]:
        gain = gain * one(*cut)
    return gain


def scatter_about(stream_key, shape, spread, bound, split=(), dtype=jnp.bfloat16):
    values = spread * jax.random.normal(stream_key, shape, jnp.float32)
    if split:
        values = values * level_of(stream_key, shape, split, -0.22, 0.18)
    return jnp.clip(values, -bound, bound).astype(dtype)


def setup_inputs(seed: int = 0) -> dict:
    streams_of = jax.random.split(jax.random.key(seed), 10)
    tokens = scatter_about(streams_of[0], (TOKENS, D), 1.0, 6.0, ((0, 32),))
    norm_gain1 = jnp.clip(1.0 + 0.18 * jax.random.normal(streams_of[1], (D,), jnp.float32), 0.1, 1.9)
    in_weight = scatter_about(streams_of[2], (D, 3, D), D ** -0.5, 0.1875, ((0, 16), (2, 2)))
    conv_kernel = scatter_about(streams_of[3], (3, D), 3 ** -0.5, 3.5, ((1, 2),))
    out_weight = scatter_about(streams_of[4], (D, D), D ** -0.5, 0.1875, ((0, 16), (1, 2)))
    norm_gain2 = jnp.clip(1.0 + 0.18 * jax.random.normal(streams_of[5], (D,), jnp.float32), 0.1, 1.9)
    gate_up_weight = scatter_about(streams_of[6], (D, 2, FF), D ** -0.5, 0.1875, ((0, 16), (2, 2)))
    down_weight = scatter_about(streams_of[7], (D, FF), FF ** -0.5, 0.09375, ((0, 16), (1, 2)))
    out_grad = scatter_about(streams_of[8], (TOKENS, D), 1.0, 6.0, ((0, 32),))
    return {"tokens": tokens, "norm_gain1": norm_gain1, "in_weight": in_weight, "conv_kernel": conv_kernel, "out_weight": out_weight, "norm_gain2": norm_gain2, "gate_up_weight": gate_up_weight, "down_weight": down_weight, "out_grad": out_grad}


eps = 1e-05
highest = lax.Precision.HIGHEST

@jax.custom_vjp
def low(v):
    return lax.optimization_barrier(v.astype(jnp.bfloat16)).astype(jnp.float32)

@jax.custom_vjp
def low_back(v):
    return v

def low_keep(v):
    return (low(v), None)

def low_pass(kept, grad):
    return (grad,)

def back_keep(v):
    return (v, None)

def back_low(kept, grad):
    return (low(grad),)
low.defvjp(low_keep, low_pass)
low_back.defvjp(back_keep, back_low)

def rms_scale(values, norm_gain):
    return values * lax.rsqrt(lax.optimization_barrier(jnp.mean(values * values, axis=-1, keepdims=True)) + eps) * norm_gain

def causal_conv(values, kernel):
    channels = values.shape[-1]
    blocks = values.reshape(-1, LEN, channels)
    padded = jnp.pad(blocks, ((0, 0), (2, 0), (0, 0)))
    summed = kernel[0] * padded[:, 0:LEN] + kernel[1] * padded[:, 1:LEN + 1] + kernel[2] * padded[:, 2:LEN + 2]
    return summed.reshape(values.shape)

def forward(stream, norm_gain1, in_weight, conv_kernel, out_weight, norm_gain2, gate_up_weight, down_weight):
    normed1 = low(rms_scale(stream, norm_gain1))
    projected = low_back(jnp.einsum('td,dkc->tkc', normed1, in_weight, precision=highest))
    mixed_in = projected[:, 0] * projected[:, 2]
    convolved = causal_conv(mixed_in, conv_kernel)
    gated = low(projected[:, 1] * convolved)
    branch_one = low_back(jnp.einsum('tc,jc->tj', gated, out_weight, precision=highest))
    middle = stream + branch_one
    normed2 = low(rms_scale(middle, norm_gain2))
    gate_up = low_back(jnp.einsum('td,dkf->tkf', normed2, gate_up_weight, precision=highest))
    hidden = low(jax.nn.silu(gate_up[:, 0]) * gate_up[:, 1])
    branch_two = low_back(jnp.einsum('tf,jf->tj', hidden, down_weight, precision=highest))
    return middle + branch_two

def reference(tokens, norm_gain1, in_weight, conv_kernel, out_weight, norm_gain2, gate_up_weight, down_weight, out_grad):
    weights = (norm_gain1.astype(jnp.float32), in_weight.astype(jnp.float32), conv_kernel.astype(jnp.float32), out_weight.astype(jnp.float32), norm_gain2.astype(jnp.float32), gate_up_weight.astype(jnp.float32), down_weight.astype(jnp.float32))
    group_rows = TOK_DEV * N_TENSOR
    groups = TOKENS // group_rows
    stream = tokens.astype(jnp.float32).reshape(groups, group_rows, D)
    cotangent = out_grad.astype(jnp.float32).reshape(groups, group_rows, D)

    def one_group(totals, pieces):
        block, block_grad = pieces
        result, pullback = jax.vjp(forward, block, *weights)
        grads = pullback(block_grad)
        totals = tuple((total + grad for total, grad in zip(totals, grads[1:])))
        return (totals, (result, grads[0]))
    zeros = tuple((jnp.zeros_like(weight) for weight in weights))
    totals, outputs = lax.scan(one_group, zeros, (stream, cotangent))
    results, input_grads = outputs
    return (results.reshape(TOKENS, D).astype(jnp.bfloat16), input_grads.reshape(TOKENS, D), totals[0], totals[1], totals[2], totals[3], totals[4], totals[5], totals[6])
```

```python
import jax
import jax.numpy as jnp
from jax import lax
from jax.sharding import PartitionSpec as P

LEN = 1024


eps = 1e-05


def rms_forward(stream, norm_gain):
    inverse = lax.rsqrt(jnp.mean(stream * stream, axis=-1, keepdims=True) + eps)
    unit_rows = stream * inverse
    return (unit_rows * norm_gain, unit_rows, inverse)


def rms_backward(grad_normed, unit_rows, inverse, norm_gain):
    gain_grad = jnp.sum(grad_normed * unit_rows, axis=0)
    grad_unit = grad_normed * norm_gain
    along = jnp.mean(grad_unit * unit_rows, axis=-1, keepdims=True)
    return (inverse * (grad_unit - unit_rows * along), gain_grad)


def causal_conv(values, kernel):
    channels = values.shape[-1]
    blocks = values.reshape(-1, LEN, channels)
    padded = jnp.pad(blocks, ((0, 0), (2, 0), (0, 0)))
    summed = (
        kernel[0] * padded[:, 0:LEN]
        + kernel[1] * padded[:, 1 : LEN + 1]
        + kernel[2] * padded[:, 2 : LEN + 2]
    )
    return summed.reshape(values.shape)


def conv_backward(grad_out, values, kernel):
    channels = values.shape[-1]
    grad_blocks = grad_out.reshape(-1, LEN, channels)
    padded = jnp.pad(values.reshape(-1, LEN, channels), ((0, 0), (2, 0), (0, 0)))
    kernel_grad = jnp.stack(
        [
            jnp.sum(grad_blocks * padded[:, 0:LEN], axis=(0, 1)),
            jnp.sum(grad_blocks * padded[:, 1 : LEN + 1], axis=(0, 1)),
            jnp.sum(grad_blocks * padded[:, 2 : LEN + 2], axis=(0, 1)),
        ]
    )
    later = jnp.pad(grad_blocks, ((0, 0), (0, 2), (0, 0)))
    grad_values = (
        kernel[0] * later[:, 2 : LEN + 2]
        + kernel[1] * later[:, 1 : LEN + 1]
        + kernel[2] * later[:, 0:LEN]
    )
    return (grad_values.reshape(values.shape), kernel_grad)


def mixer_forward(normed_rows, in_w, kernel):
    projected = jnp.einsum("td,dkc->tkc", normed_rows, in_w, preferred_element_type=jnp.float32)
    mixed_in = projected[:, 0] * projected[:, 2]
    convolved = causal_conv(mixed_in, kernel)
    gated = (projected[:, 1] * convolved).astype(jnp.bfloat16)
    return (projected, mixed_in, convolved, gated)


def mixer_backward(grad_gated, projected, mixed_in, convolved, kernel):
    grad_c = grad_gated * convolved
    grad_conv = grad_gated * projected[:, 1]
    grad_mixed, kernel_grad = conv_backward(grad_conv, mixed_in, kernel)
    grad_stack = jnp.stack(
        [grad_mixed * projected[:, 2], grad_c, grad_mixed * projected[:, 0]], axis=1
    )
    return (grad_stack.astype(jnp.bfloat16), kernel_grad)


def ffn_forward(normed_rows, gate_up_w):
    gate_up = jnp.einsum("td,dkf->tkf", normed_rows, gate_up_w, preferred_element_type=jnp.float32)
    hidden = (jax.nn.silu(gate_up[:, 0]) * gate_up[:, 1]).astype(jnp.bfloat16)
    return (gate_up, hidden)


def ffn_backward(grad_hidden, gate_up):
    gate = gate_up[:, 0]
    sigm = jax.nn.sigmoid(gate)
    grad_up = grad_hidden * gate * sigm
    grad_gate = grad_hidden * gate_up[:, 1] * sigm * (1.0 + gate * (1.0 - sigm))
    return jnp.stack([grad_gate, grad_up], axis=1).astype(jnp.bfloat16)


def run_layer(
    tokens,
    out_grad,
    gain_one,
    gain_two,
    in_w,
    kernel_b,
    out_w,
    gate_up_w,
    down_w,
    mixer_movers,
    ffn_movers,
):
    collect_first, reduce_first, collect_grad1, reduce_back1 = mixer_movers
    collect_second, reduce_second, reduce_back2 = ffn_movers
    own_rows = tokens.shape[0]
    kernel = kernel_b.astype(jnp.float32)
    stream = tokens.astype(jnp.float32)
    normed1, unit1, inverse1 = rms_forward(stream, gain_one)
    group_n1 = collect_first(normed1.astype(jnp.bfloat16))
    projected, mixed_in, convolved, gated = mixer_forward(group_n1, in_w, kernel)

    def mix_term(first_row, row_count):
        return jnp.einsum("tc,jc->tj", gated, out_w, preferred_element_type=jnp.float32)

    middle = stream + reduce_first(mix_term, own_rows)
    normed2, unit2, inverse2 = rms_forward(middle, gain_two)
    group_n2, group_grad = collect_second((normed2.astype(jnp.bfloat16), out_grad))
    gate_up, hidden = ffn_forward(group_n2, gate_up_w)

    def ffn_term(first_row, row_count):
        return jnp.einsum("tf,jf->tj", hidden, down_w, preferred_element_type=jnp.float32)

    result = (middle + reduce_second(ffn_term, own_rows)).astype(jnp.bfloat16)
    grad_hidden = jnp.dot(group_grad, down_w, preferred_element_type=jnp.float32)
    down_grad_w = jnp.einsum("tj,tf->jf", group_grad, hidden, preferred_element_type=jnp.float32)
    grad_gate_up = ffn_backward(grad_hidden, gate_up)
    gate_up_grad_w = jnp.einsum(
        "td,tkf->dkf", group_n2, grad_gate_up, preferred_element_type=jnp.float32
    )

    def ffn_back_term(first_row, row_count):
        return jnp.einsum(
            "tkf,dkf->td", grad_gate_up, gate_up_w, preferred_element_type=jnp.float32
        )

    grad_normed2 = reduce_back2(ffn_back_term, own_rows)
    grad_rms2, gain_two_grad = rms_backward(grad_normed2, unit2, inverse2, gain_two)
    grad_middle = out_grad.astype(jnp.float32) + grad_rms2
    group_gm = collect_grad1(grad_middle.astype(jnp.bfloat16))
    out_grad_w = jnp.einsum("tj,tc->jc", group_gm, gated, preferred_element_type=jnp.float32)
    grad_gated = jnp.einsum("tj,jc->tc", group_gm, out_w, preferred_element_type=jnp.float32)
    grad_projected, kernel_grad = mixer_backward(grad_gated, projected, mixed_in, convolved, kernel)
    in_grad_w = jnp.einsum(
        "td,tkc->dkc", group_n1, grad_projected, preferred_element_type=jnp.float32
    )

    def mixer_back_term(first_row, row_count):
        return jnp.einsum("tkc,dkc->td", grad_projected, in_w, preferred_element_type=jnp.float32)

    grad_normed1 = reduce_back1(mixer_back_term, own_rows)
    grad_rms1, gain_one_grad = rms_backward(grad_normed1, unit1, inverse1, gain_one)
    input_grad = grad_middle + grad_rms1
    return (
        result,
        input_grad,
        (gain_one_grad, gain_two_grad),
        (in_grad_w, out_grad_w),
        (gate_up_grad_w, down_grad_w),
        kernel_grad,
    )


def per_device(
    tokens,
    norm_gain1,
    in_weight,
    conv_kernel,
    out_weight,
    norm_gain2,
    gate_up_weight,
    down_weight,
    out_grad,
):
    channels = in_weight.shape[2]
    model_width = tokens.shape[1]
    in_part, out_part, gate_up_part, down_part = (
        lax.all_gather(in_weight, "dp", axis=0, tiled=True),
        lax.all_gather(out_weight, "dp", axis=0, tiled=True),
        lax.all_gather(gate_up_weight, "dp", axis=0, tiled=True),
        lax.all_gather(down_weight, "dp", axis=0, tiled=True),
    )
    in_use, out_use, kernel_use = (in_part, out_part, conv_kernel)

    def collect_first(values):
        return lax.all_gather(values, "tensor", axis=0, tiled=True)

    def reduce_first(term_fn, row_count):
        return lax.psum_scatter(
            term_fn(jnp.int32(0), lax.axis_size("tensor") * row_count),
            "tensor",
            scatter_dimension=0,
            tiled=True,
        )

    def collect_grad1(values):
        return lax.all_gather(values, "tensor", axis=0, tiled=True)

    def reduce_back1(term_fn, row_count):
        return lax.psum_scatter(
            term_fn(jnp.int32(0), lax.axis_size("tensor") * row_count),
            "tensor",
            scatter_dimension=0,
            tiled=True,
        )

    mixer_movers = (collect_first, reduce_first, collect_grad1, reduce_back1)
    gate_up_use, down_use = (gate_up_part, down_part)

    def collect_second(values):
        return (
            lax.all_gather(values[0], "tensor", axis=0, tiled=True),
            lax.all_gather(values[1], "tensor", axis=0, tiled=True),
        )

    def reduce_second(term_fn, row_count):
        return lax.psum_scatter(
            term_fn(jnp.int32(0), lax.axis_size("tensor") * row_count),
            "tensor",
            scatter_dimension=0,
            tiled=True,
        )

    def reduce_back2(term_fn, row_count):
        return lax.psum_scatter(
            term_fn(jnp.int32(0), lax.axis_size("tensor") * row_count),
            "tensor",
            scatter_dimension=0,
            tiled=True,
        )

    ffn_movers = (collect_second, reduce_second, reduce_back2)
    result, input_grad, gain_grads, mixer_grads, ffn_grads, kernel_grad = run_layer(
        tokens,
        out_grad,
        norm_gain1,
        norm_gain2,
        in_use,
        kernel_use,
        out_use,
        gate_up_use,
        down_use,
        mixer_movers,
        ffn_movers,
    )
    in_share, out_share = mixer_grads
    offset = lax.axis_index("tensor") * channels
    kernel_full = lax.dynamic_update_slice(
        jnp.zeros((3, model_width), jnp.float32), kernel_grad, (jnp.int32(0), offset)
    )
    gate_up_share, down_share = ffn_grads
    in_final, out_final, gate_up_final, down_final = (
        lax.psum_scatter(in_share, "dp", scatter_dimension=0, tiled=True),
        lax.psum_scatter(out_share, "dp", scatter_dimension=0, tiled=True),
        lax.psum_scatter(gate_up_share, "dp", scatter_dimension=0, tiled=True),
        lax.psum_scatter(down_share, "dp", scatter_dimension=0, tiled=True),
    )
    gain_one_sum, gain_two_sum, kernel_sum = lax.psum(
        (gain_grads[0], gain_grads[1], kernel_full), ("dp", "tensor")
    )
    conv_share = lax.dynamic_slice_in_dim(
        kernel_sum, lax.axis_index("tensor") * channels, channels, 1
    )
    return (
        result,
        input_grad,
        gain_one_sum,
        in_final,
        conv_share,
        out_final,
        gain_two_sum,
        gate_up_final,
        down_final,
    )


def exchange(values):
    return lax.ppermute(values, "tensor", [(0, 1), (1, 0)])


def across(values, bit):
    return lax.ppermute(values, "dp", [(place, place ^ bit) for place in range(16)])


def line_step(values, first, last, shift):
    return lax.ppermute(
        values,
        "dp",
        [(place, place + 4 * shift) for place in range(16) if first <= place // 4 <= last],
    )


def place_bits():
    place = lax.axis_index("dp")
    return place // 4, (place // 2) % 2, place % 2


def gather_line(values, axis):
    upward, downward, ups, downs = values, values, [], []
    for step in range(3):
        upward = line_step(upward, step, 2, 1)
        downward = line_step(downward, 1, 3 - step, -1)
        ups.append(upward)
        downs.append(downward)
    line = jnp.stack(ups[::-1] + [values] + downs, axis)
    return lax.dynamic_slice_in_dim(line, 3 - place_bits()[0], 4, axis)


def gather_pair(values, bit, axis):
    other = across(values, bit)
    own_bit = place_bits()[2 if bit == 1 else 1]
    return jnp.where(
        own_bit == 0, jnp.stack([values, other], axis), jnp.stack([other, values], axis)
    )


def add_wide(first, second):
    return first.astype(jnp.float32) + second.astype(jnp.float32)


def reduce_pair(values, bit, axis):
    own_bit = place_bits()[2 if bit == 1 else 1]
    other = across(lax.dynamic_index_in_dim(values, 1 - own_bit, axis, keepdims=False), bit)
    own = lax.dynamic_index_in_dim(values, own_bit, axis, keepdims=False)
    return add_wide(own, other)


def reduce_line(values, axis):
    level = place_bits()[0]

    def part(index):
        return lax.dynamic_index_in_dim(values, jnp.clip(index, 0, 3), axis, keepdims=False)

    upward, downward = None, None
    for step in range(3):
        up_part, down_part = part(3 - step + level), part(step - 3 + level)
        if step:
            up_part = add_wide(up_part, upward).astype(jnp.bfloat16)
            down_part = add_wide(down_part, downward).astype(jnp.bfloat16)
        upward = line_step(up_part, 0, min(step, 2), 1)
        downward = line_step(down_part, max(3 - step, 1), 3, -1)
    return add_wide(part(level), upward) + downward.astype(jnp.float32)


def gather_mixer(in_weight, out_weight):
    kinds = jnp.concatenate([jnp.transpose(in_weight, (1, 0, 2)), out_weight[None]], 0)
    lines = gather_line(kinds, 1)
    first = gather_pair(gather_pair(lines[:2], 2, 2), 1, 3)
    second = gather_pair(gather_pair(lines[2:], 1, 2), 2, 2)
    rows = 16 * in_weight.shape[0]
    return first.reshape(2, rows, -1), second.reshape(2, rows, -1)


def gather_gate_up(gate_up_weight):
    lines = gather_line(jnp.transpose(gate_up_weight, (1, 0, 2)), 1)
    gate = gather_pair(gather_pair(lines[0], 2, 1), 1, 2)
    up = gather_pair(gather_pair(lines[1], 1, 1), 2, 1)
    rows = 16 * gate_up_weight.shape[0]
    return gate.reshape(rows, -1), up.reshape(rows, -1)


def gather_down(down_weight):
    half = down_weight.shape[0] // 2
    first = gather_pair(gather_pair(down_weight[:half], 2, 0), 1, 1)
    second = gather_pair(gather_pair(down_weight[half:], 1, 0), 2, 0)
    lines = gather_line(jnp.concatenate([first, second], 2), 0)
    return lines.reshape(16 * down_weight.shape[0], -1)


def narrow(values):
    return values.astype(jnp.bfloat16)


def scatter_first(grad):
    parts = grad.reshape(4, 2, 2, grad.shape[0] // 16, grad.shape[1])
    return reduce_line(narrow(reduce_pair(narrow(reduce_pair(parts, 1, 2)), 2, 1)), 0)


def scatter_second(grad):
    parts = grad.reshape(4, 2, 2, grad.shape[0] // 16, grad.shape[1])
    return reduce_line(narrow(reduce_pair(narrow(reduce_pair(parts, 2, 1)), 1, 1)), 0)


def scatter_down(grad):
    rows = grad.shape[0] // 16
    parts = narrow(reduce_line(grad.reshape(4, 2, 2, rows, grad.shape[1]), 0))
    first, second = parts[:, :, : rows // 2], parts[:, :, rows // 2 :]
    first = reduce_pair(narrow(reduce_pair(first, 1, 1)), 2, 0)
    second = reduce_pair(narrow(reduce_pair(second, 2, 0)), 1, 0)
    return jnp.concatenate([first, second], 0)


def sum_all(values):
    for bit in (1, 2, 4, 8):
        values = values + across(values, bit)
    return values


def per_device_pairs(
    tokens,
    norm_gain1,
    in_weight,
    conv_kernel,
    out_weight,
    norm_gain2,
    gate_up_weight,
    down_weight,
    out_grad,
):
    rows = tokens.shape[0]
    dot = lambda spec, a, b: jnp.einsum(spec, a, b, preferred_element_type=jnp.float32)
    collect = lambda values: jnp.concatenate([values, exchange(values)], 0)
    merge = lambda values: values[:rows] + exchange(narrow(values[rows:])).astype(jnp.float32)
    kernel = conv_kernel.astype(jnp.float32)
    (w_b, w_c), (w_x, w_out) = gather_mixer(in_weight, out_weight)
    w_down = gather_down(down_weight)
    w_gate, w_up = gather_gate_up(gate_up_weight)
    group_grad = collect(out_grad)
    stream = tokens.astype(jnp.float32)
    normed1, unit1, inverse1 = rms_forward(stream, norm_gain1)
    group_n1 = collect(narrow(normed1))
    b_rows, c_rows, x_rows = (dot("td,dc->tc", group_n1, w) for w in (w_b, w_c, w_x))
    mixed_in = b_rows * x_rows
    convolved = causal_conv(mixed_in, kernel)
    gated = narrow(c_rows * convolved)
    middle = stream + merge(dot("tc,jc->tj", gated, w_out))
    normed2, unit2, inverse2 = rms_forward(middle, norm_gain2)
    group_n2 = collect(narrow(normed2))
    grad_hidden = dot("tj,jf->tf", group_grad, w_down)
    gate = dot("td,df->tf", group_n2, w_gate)
    up = dot("td,df->tf", group_n2, w_up)
    sigm = jax.nn.sigmoid(gate)
    hidden = narrow(gate * sigm * up)
    grad_up = narrow(grad_hidden * gate * sigm)
    grad_gate = narrow(grad_hidden * up * sigm * (1.0 + gate * (1.0 - sigm)))
    down_final = scatter_down(narrow(dot("tj,tf->jf", group_grad, hidden)))
    gate_final = scatter_first(narrow(dot("td,tf->df", group_n2, grad_gate)))
    up_final = scatter_second(narrow(dot("td,tf->df", group_n2, grad_up)))
    grad_normed2 = merge(
        dot("tf,df->td", grad_gate, w_gate) + dot("tf,df->td", grad_up, w_up)
    )
    result = narrow(middle + merge(dot("tf,jf->tj", hidden, w_down)))
    grad_rms2, gain_two_grad = rms_backward(grad_normed2, unit2, inverse2, norm_gain2)
    grad_middle = out_grad.astype(jnp.float32) + grad_rms2
    group_gm = collect(narrow(grad_middle))
    grad_gated = dot("tj,jc->tc", group_gm, w_out)
    out_final = scatter_second(narrow(dot("tj,tc->jc", group_gm, gated)))
    grad_c = narrow(grad_gated * convolved)
    grad_mixed, kernel_grad = conv_backward(grad_gated * c_rows, mixed_in, kernel)
    grad_b, grad_x = narrow(grad_mixed * x_rows), narrow(grad_mixed * b_rows)
    b_final = scatter_first(narrow(dot("td,tc->dc", group_n1, grad_b)))
    c_final = scatter_first(narrow(dot("td,tc->dc", group_n1, grad_c)))
    x_final = scatter_second(narrow(dot("td,tc->dc", group_n1, grad_x)))
    grad_normed1 = merge(
        dot("tc,dc->td", grad_b, w_b)
        + dot("tc,dc->td", grad_c, w_c)
        + dot("tc,dc->td", grad_x, w_x)
    )
    grad_rms1, gain_one_grad = rms_backward(grad_normed1, unit1, inverse1, norm_gain1)
    input_grad = grad_middle + grad_rms1
    summed = sum_all(jnp.concatenate([gain_one_grad, gain_two_grad, kernel_grad.reshape(-1)]))
    width = gain_one_grad.shape[0]
    gains = summed[: 2 * width]
    gains = gains + exchange(gains)
    return (
        result,
        input_grad,
        gains[:width],
        jnp.stack([b_final, c_final, x_final], 1),
        summed[2 * width :].reshape(kernel_grad.shape),
        out_final,
        gains[width:],
        jnp.stack([gate_final, up_final], 1),
        down_final,
    )


def solution(mesh):
    paired = mesh.shape["dp"] == 16 and mesh.shape["tensor"] == 2
    return jax.shard_map(
        per_device_pairs if paired else per_device,
        mesh=mesh,
        in_specs=(
            P(("dp", "tensor"), None),
            P(),
            P("dp", None, "tensor"),
            P(None, "tensor"),
            P("dp", "tensor"),
            P(),
            P("dp", None, "tensor"),
            P("dp", "tensor"),
            P(("dp", "tensor"), None),
        ),
        out_specs=(
            P(("dp", "tensor"), None),
            P(("dp", "tensor"), None),
            P(),
            P("dp", None, "tensor"),
            P(None, "tensor"),
            P("dp", "tensor"),
            P(),
            P("dp", None, "tensor"),
            P("dp", "tensor"),
        ),
        check_vma=False,
    )
```

```python
import functools

import jax
import jax.numpy as jnp
from jax import lax
from jax.experimental import pallas as pl
from jax.experimental.pallas import tpu as pltpu
from jax.sharding import PartitionSpec as P

LEN = 1024


eps = 1e-05


def rms_forward(stream, norm_gain):
    inverse = lax.rsqrt(jnp.mean(stream * stream, axis=-1, keepdims=True) + eps)
    unit_rows = stream * inverse
    return (unit_rows * norm_gain, unit_rows, inverse)


def rms_backward(grad_normed, unit_rows, inverse, norm_gain):
    gain_grad = jnp.sum(grad_normed * unit_rows, axis=0)
    grad_unit = grad_normed * norm_gain
    along = jnp.mean(grad_unit * unit_rows, axis=-1, keepdims=True)
    return (inverse * (grad_unit - unit_rows * along), gain_grad)


def causal_conv(values, kernel):
    channels = values.shape[-1]
    blocks = values.reshape(-1, LEN, channels)
    padded = jnp.pad(blocks, ((0, 0), (2, 0), (0, 0)))
    summed = (
        kernel[0] * padded[:, 0:LEN]
        + kernel[1] * padded[:, 1 : LEN + 1]
        + kernel[2] * padded[:, 2 : LEN + 2]
    )
    return summed.reshape(values.shape)


def conv_backward(grad_out, values, kernel):
    channels = values.shape[-1]
    grad_blocks = grad_out.reshape(-1, LEN, channels)
    padded = jnp.pad(values.reshape(-1, LEN, channels), ((0, 0), (2, 0), (0, 0)))
    kernel_grad = jnp.stack(
        [
            jnp.sum(grad_blocks * padded[:, 0:LEN], axis=(0, 1)),
            jnp.sum(grad_blocks * padded[:, 1 : LEN + 1], axis=(0, 1)),
            jnp.sum(grad_blocks * padded[:, 2 : LEN + 2], axis=(0, 1)),
        ]
    )
    later = jnp.pad(grad_blocks, ((0, 0), (0, 2), (0, 0)))
    grad_values = (
        kernel[0] * later[:, 2 : LEN + 2]
        + kernel[1] * later[:, 1 : LEN + 1]
        + kernel[2] * later[:, 0:LEN]
    )
    return (grad_values.reshape(values.shape), kernel_grad)


def mixer_forward(normed_rows, in_w, kernel):
    projected = jnp.einsum("td,dkc->tkc", normed_rows, in_w, preferred_element_type=jnp.float32)
    mixed_in = projected[:, 0] * projected[:, 2]
    convolved = causal_conv(mixed_in, kernel)
    gated = (projected[:, 1] * convolved).astype(jnp.bfloat16)
    return (projected, mixed_in, convolved, gated)


def mixer_backward(grad_gated, projected, mixed_in, convolved, kernel):
    grad_c = grad_gated * convolved
    grad_conv = grad_gated * projected[:, 1]
    grad_mixed, kernel_grad = conv_backward(grad_conv, mixed_in, kernel)
    grad_stack = jnp.stack(
        [grad_mixed * projected[:, 2], grad_c, grad_mixed * projected[:, 0]], axis=1
    )
    return (grad_stack.astype(jnp.bfloat16), kernel_grad)


def ffn_forward(normed_rows, gate_up_w):
    gate_up = jnp.einsum("td,dkf->tkf", normed_rows, gate_up_w, preferred_element_type=jnp.float32)
    hidden = (jax.nn.silu(gate_up[:, 0]) * gate_up[:, 1]).astype(jnp.bfloat16)
    return (gate_up, hidden)


def ffn_backward(grad_hidden, gate_up):
    gate = gate_up[:, 0]
    sigm = jax.nn.sigmoid(gate)
    grad_up = grad_hidden * gate * sigm
    grad_gate = grad_hidden * gate_up[:, 1] * sigm * (1.0 + gate * (1.0 - sigm))
    return jnp.stack([grad_gate, grad_up], axis=1).astype(jnp.bfloat16)


def run_layer(
    tokens,
    out_grad,
    gain_one,
    gain_two,
    in_w,
    kernel_b,
    out_w,
    gate_up_w,
    down_w,
    mixer_movers,
    ffn_movers,
):
    collect_first, reduce_first, collect_grad1, reduce_back1 = mixer_movers
    collect_second, reduce_second, reduce_back2 = ffn_movers
    own_rows = tokens.shape[0]
    kernel = kernel_b.astype(jnp.float32)
    stream = tokens.astype(jnp.float32)
    normed1, unit1, inverse1 = rms_forward(stream, gain_one)
    group_n1 = collect_first(normed1.astype(jnp.bfloat16))
    projected, mixed_in, convolved, gated = mixer_forward(group_n1, in_w, kernel)

    def mix_term(first_row, row_count):
        return jnp.einsum("tc,jc->tj", gated, out_w, preferred_element_type=jnp.float32)

    middle = stream + reduce_first(mix_term, own_rows)
    normed2, unit2, inverse2 = rms_forward(middle, gain_two)
    group_n2, group_grad = collect_second((normed2.astype(jnp.bfloat16), out_grad))
    gate_up, hidden = ffn_forward(group_n2, gate_up_w)

    def ffn_term(first_row, row_count):
        return jnp.einsum("tf,jf->tj", hidden, down_w, preferred_element_type=jnp.float32)

    result = (middle + reduce_second(ffn_term, own_rows)).astype(jnp.bfloat16)
    grad_hidden = jnp.dot(group_grad, down_w, preferred_element_type=jnp.float32)
    down_grad_w = jnp.einsum("tj,tf->jf", group_grad, hidden, preferred_element_type=jnp.float32)
    grad_gate_up = ffn_backward(grad_hidden, gate_up)
    gate_up_grad_w = jnp.einsum(
        "td,tkf->dkf", group_n2, grad_gate_up, preferred_element_type=jnp.float32
    )

    def ffn_back_term(first_row, row_count):
        return jnp.einsum(
            "tkf,dkf->td", grad_gate_up, gate_up_w, preferred_element_type=jnp.float32
        )

    grad_normed2 = reduce_back2(ffn_back_term, own_rows)
    grad_rms2, gain_two_grad = rms_backward(grad_normed2, unit2, inverse2, gain_two)
    grad_middle = out_grad.astype(jnp.float32) + grad_rms2
    group_gm = collect_grad1(grad_middle.astype(jnp.bfloat16))
    out_grad_w = jnp.einsum("tj,tc->jc", group_gm, gated, preferred_element_type=jnp.float32)
    grad_gated = jnp.einsum("tj,jc->tc", group_gm, out_w, preferred_element_type=jnp.float32)
    grad_projected, kernel_grad = mixer_backward(grad_gated, projected, mixed_in, convolved, kernel)
    in_grad_w = jnp.einsum(
        "td,tkc->dkc", group_n1, grad_projected, preferred_element_type=jnp.float32
    )

    def mixer_back_term(first_row, row_count):
        return jnp.einsum("tkc,dkc->td", grad_projected, in_w, preferred_element_type=jnp.float32)

    grad_normed1 = reduce_back1(mixer_back_term, own_rows)
    grad_rms1, gain_one_grad = rms_backward(grad_normed1, unit1, inverse1, gain_one)
    input_grad = grad_middle + grad_rms1
    return (
        result,
        input_grad,
        (gain_one_grad, gain_two_grad),
        (in_grad_w, out_grad_w),
        (gate_up_grad_w, down_grad_w),
        kernel_grad,
    )


def per_device(
    tokens,
    norm_gain1,
    in_weight,
    conv_kernel,
    out_weight,
    norm_gain2,
    gate_up_weight,
    down_weight,
    out_grad,
):
    channels = in_weight.shape[2]
    model_width = tokens.shape[1]
    in_part, out_part, gate_up_part, down_part = (
        lax.all_gather(in_weight, "dp", axis=0, tiled=True),
        lax.all_gather(out_weight, "dp", axis=0, tiled=True),
        lax.all_gather(gate_up_weight, "dp", axis=0, tiled=True),
        lax.all_gather(down_weight, "dp", axis=0, tiled=True),
    )
    in_use, out_use, kernel_use = (in_part, out_part, conv_kernel)

    def collect_first(values):
        return lax.all_gather(values, "tensor", axis=0, tiled=True)

    def reduce_first(term_fn, row_count):
        return lax.psum_scatter(
            term_fn(jnp.int32(0), lax.axis_size("tensor") * row_count),
            "tensor",
            scatter_dimension=0,
            tiled=True,
        )

    def collect_grad1(values):
        return lax.all_gather(values, "tensor", axis=0, tiled=True)

    def reduce_back1(term_fn, row_count):
        return lax.psum_scatter(
            term_fn(jnp.int32(0), lax.axis_size("tensor") * row_count),
            "tensor",
            scatter_dimension=0,
            tiled=True,
        )

    mixer_movers = (collect_first, reduce_first, collect_grad1, reduce_back1)
    gate_up_use, down_use = (gate_up_part, down_part)

    def collect_second(values):
        return (
            lax.all_gather(values[0], "tensor", axis=0, tiled=True),
            lax.all_gather(values[1], "tensor", axis=0, tiled=True),
        )

    def reduce_second(term_fn, row_count):
        return lax.psum_scatter(
            term_fn(jnp.int32(0), lax.axis_size("tensor") * row_count),
            "tensor",
            scatter_dimension=0,
            tiled=True,
        )

    def reduce_back2(term_fn, row_count):
        return lax.psum_scatter(
            term_fn(jnp.int32(0), lax.axis_size("tensor") * row_count),
            "tensor",
            scatter_dimension=0,
            tiled=True,
        )

    ffn_movers = (collect_second, reduce_second, reduce_back2)
    result, input_grad, gain_grads, mixer_grads, ffn_grads, kernel_grad = run_layer(
        tokens,
        out_grad,
        norm_gain1,
        norm_gain2,
        in_use,
        kernel_use,
        out_use,
        gate_up_use,
        down_use,
        mixer_movers,
        ffn_movers,
    )
    in_share, out_share = mixer_grads
    offset = lax.axis_index("tensor") * channels
    kernel_full = lax.dynamic_update_slice(
        jnp.zeros((3, model_width), jnp.float32), kernel_grad, (jnp.int32(0), offset)
    )
    gate_up_share, down_share = ffn_grads
    in_final, out_final, gate_up_final, down_final = (
        lax.psum_scatter(in_share, "dp", scatter_dimension=0, tiled=True),
        lax.psum_scatter(out_share, "dp", scatter_dimension=0, tiled=True),
        lax.psum_scatter(gate_up_share, "dp", scatter_dimension=0, tiled=True),
        lax.psum_scatter(down_share, "dp", scatter_dimension=0, tiled=True),
    )
    gain_one_sum, gain_two_sum, kernel_sum = lax.psum(
        (gain_grads[0], gain_grads[1], kernel_full), ("dp", "tensor")
    )
    conv_share = lax.dynamic_slice_in_dim(
        kernel_sum, lax.axis_index("tensor") * channels, channels, 1
    )
    return (
        result,
        input_grad,
        gain_one_sum,
        in_final,
        conv_share,
        out_final,
        gain_two_sum,
        gate_up_final,
        down_final,
    )


def exchange(values):
    return lax.ppermute(values, "tensor", [(0, 1), (1, 0)])


def across(values, bit):
    return lax.ppermute(values, "dp", [(place, place ^ bit) for place in range(16)])


def between(values, steps):
    pairs = [
        (place, place + 4 * shift)
        for level, shift in steps
        for place in range(4 * level, 4 * level + 4)
    ]
    return lax.ppermute(values, "dp", pairs)


def place_bits():
    place = lax.axis_index("dp")
    return place // 4, (place // 2) % 2, place % 2


def in_order(own_bit, own, other):
    return jnp.where(
        own_bit == 0, jnp.concatenate([own, other], 0), jnp.concatenate([other, own], 0)
    )


def tie(*values):
    return lax.optimization_barrier(values)


def add_wide(first, second):
    return first.astype(jnp.float32) + second.astype(jnp.float32)


def narrow(values):
    return values.astype(jnp.bfloat16)


def gather_direct(values):
    ups = [between(values, [(z, s) for z in range(4 - s)]) for s in (1, 2, 3)]
    downs = [between(values, [(z, -s) for z in range(s, 4)]) for s in (1, 2, 3)]
    line = jnp.stack(ups[::-1] + [values] + downs)
    return lax.dynamic_slice_in_dim(line, 3 - place_bits()[0], 4, 0)


def line_near(values):
    return in_order(place_bits()[0] % 2, values[None], across(values, 4)[None])


def line_middle(near):
    return between(near, [(1, 1), (2, -1)])


def line_far(near, middle):
    level = place_bits()[0]
    outer = between(middle, [(1, -1), (2, 1)])
    far = jnp.where((level == 1) | (level == 2), middle, outer)
    return in_order(level // 2, near, far)


def gather_pair(values, bit):
    own_bit = place_bits()[2 if bit == 1 else 1]
    return in_order(own_bit, values[None], across(values, bit)[None])


def pick(values, index):
    return lax.dynamic_index_in_dim(values, index, 0, keepdims=False)


def reduce_pair(values, bit):
    own_bit = place_bits()[2 if bit == 1 else 1]
    return narrow(add_wide(pick(values, own_bit), across(pick(values, 1 - own_bit), bit)))


def reduce_far(values):
    half = place_bits()[0] // 2
    mine = lax.dynamic_slice_in_dim(values, 2 * half, 2, 0)
    theirs = lax.dynamic_slice_in_dim(values, 2 - 2 * half, 2, 0)
    return mine, narrow(add_wide(theirs, between(theirs, [(0, 1), (3, -1)])))


def reduce_middle(mine, theirs):
    return narrow(add_wide(mine, between(theirs, [(1, 1), (2, -1)])))


def reduce_near(mine):
    bit = place_bits()[0] % 2
    return add_wide(pick(mine, bit), across(pick(mine, 1 - bit), 4))


def reduce_direct(values):
    level = place_bits()[0]
    total = pick(values, level).astype(jnp.float32)
    for s in (1, 2, 3):
        upper, lower = jnp.minimum(level + s, 3), jnp.maximum(level - s, 0)
        total = total + between(pick(values, upper), [(z, s) for z in range(4 - s)]).astype(
            jnp.float32
        )
        total = total + between(pick(values, lower), [(z, -s) for z in range(s, 4)]).astype(
            jnp.float32
        )
    return total


def sum_all(values):
    for bit in (1, 2, 4, 8):
        values = values + across(values, bit)
    return values


TILE = 256
TOKEN_BLOCK = 512
ROW_BLOCK = 256
VMEM_LIMIT = 60 * 1024 * 1024


def wide_dot(left, right):
    return jnp.dot(left, right, preferred_element_type=jnp.float32)


def wide_dot_t(left, right):
    return lax.dot_general(
        left, right, (((1,), (1,)), ((), ())), preferred_element_type=jnp.float32
    )


def unit_and_inverse(rows):
    inverse = lax.rsqrt(jnp.mean(rows * rows, axis=-1, keepdims=True) + eps)
    return rows * inverse, inverse


def norm_kernel(tokens, gain, normed):
    unit, _ = unit_and_inverse(tokens[...].astype(jnp.float32))
    normed[...] = narrow(unit * gain[...])


def middle_kernel(tokens, own, other, gain, middle, normed):
    rows = tokens[...].astype(jnp.float32) + (own[...] + other[...].astype(jnp.float32))
    middle[...] = rows
    unit, _ = unit_and_inverse(rows)
    normed[...] = narrow(unit * gain[...])


def norm_back(rows, grad, gain, gain_grad):
    unit, inverse = unit_and_inverse(rows)

    @pl.when(pl.program_id(0) == 0)
    def _():
        gain_grad[...] = jnp.zeros_like(gain_grad)

    gain_grad[...] += jnp.sum(grad * unit, axis=0, keepdims=True)
    grad_unit = grad * gain
    along = jnp.mean(grad_unit * unit, axis=-1, keepdims=True)
    return inverse * (grad_unit - unit * along)


def middle_back_kernel(own, other, middle, gain, out_grad, grad_middle, narrowed, gain_grad):
    grad = own[...] + other[...].astype(jnp.float32)
    total = out_grad[...].astype(jnp.float32) + norm_back(
        middle[...], grad, gain[...], gain_grad
    )
    grad_middle[...] = total
    narrowed[...] = narrow(total)


def input_back_kernel(own, other, tokens, gain, grad_middle, input_grad, gain_grad):
    grad = own[...] + other[...].astype(jnp.float32)
    input_grad[...] = grad_middle[...] + norm_back(
        tokens[...].astype(jnp.float32), grad, gain[...], gain_grad
    )


def work(matmul_rows, depth, columns, moved):
    return pl.CostEstimate(
        flops=2 * matmul_rows * depth * columns, transcendentals=0, bytes_accessed=moved
    )


def both_kernel(own, other, group, group_t):
    half = pl.num_programs(0) // 2

    @pl.when(pl.program_id(0) < half)
    def _():
        group[...] = own[...]
        group_t[...] = own[...].T

    @pl.when(pl.program_id(0) >= half)
    def _():
        group[...] = other[...]
        group_t[...] = other[...].T


def both_call(own, other):
    rows, width = own.shape
    steps = rows // ROW_BLOCK
    return pl.pallas_call(
        both_kernel,
        out_shape=[
            jax.ShapeDtypeStruct((2 * rows, width), own.dtype),
            jax.ShapeDtypeStruct((width, 2 * rows), own.dtype),
        ],
        grid=(2 * steps,),
        in_specs=[
            pl.BlockSpec((ROW_BLOCK, width), lambda i: (jnp.minimum(i, steps - 1), 0)),
            pl.BlockSpec((ROW_BLOCK, width), lambda i: (jnp.maximum(i - steps, 0), 0)),
        ],
        out_specs=[
            pl.BlockSpec((ROW_BLOCK, width), lambda i: (i, 0)),
            pl.BlockSpec((width, ROW_BLOCK), lambda i: (0, i)),
        ],
        compiler_params=pltpu.CompilerParams(vmem_limit_bytes=VMEM_LIMIT),
        cost_estimate=work(0, 0, 0, 12 * rows * width),
        name="both",
    )(own, other)


def row_call(kernel, name, args, outs):
    tokens = args[0].shape[0]
    spec = lambda shape: (
        pl.BlockSpec((ROW_BLOCK, shape[1]), lambda i: (i, 0))
        if shape[0] == tokens
        else pl.BlockSpec(shape, lambda i: (0, 0))
    )
    return pl.pallas_call(
        kernel,
        out_shape=[jax.ShapeDtypeStruct(*out) for out in outs],
        grid=(tokens // ROW_BLOCK,),
        in_specs=[spec(arg.shape) for arg in args],
        out_specs=[spec(out[0]) for out in outs],
        compiler_params=pltpu.CompilerParams(vmem_limit_bytes=VMEM_LIMIT),
        cost_estimate=work(0, 0, 0, 16 * tokens * args[0].shape[1]),
        name=name,
    )(*args)


def place_pieces(weights, kinds, bits, first, second, first_kinds):
    x_bit, y_bit = bits[0], bits[1]
    for side in range(2):
        for z in range(4):
            for kind in range(kinds):
                if kind < first_kinds:
                    weights[kind, z, side, pl.ds(x_bit, 1)] = first[0][side, z, kind][None]
                    weights[kind, z, side, pl.ds(1 - x_bit, 1)] = first[1][side, z, kind][None]
                else:
                    at = kind - first_kinds
                    weights[kind, z, pl.ds(y_bit, 1), side] = second[0][side, z, at][None]
                    weights[kind, z, pl.ds(1 - y_bit, 1), side] = second[1][side, z, at][None]


def cut_first(product, kind, bits, send, keep, at):
    for side in range(2):
        for z in range(4):
            keep[side, z, at] = product[kind, z, side, pl.ds(bits[0], 1)][0]
            send[side, z, at] = product[kind, z, side, pl.ds(1 - bits[0], 1)][0]


def cut_second(product, kind, bits, send, keep, at):
    for side in range(2):
        for z in range(4):
            keep[side, z, at] = product[kind, z, pl.ds(bits[1], 1), side][0]
            send[side, z, at] = product[kind, z, pl.ds(1 - bits[1], 1), side][0]


def ffn_kernel(bits, normed, cotangent, normed_t, cotangent_t, shards, *rest, pairs, carried):
    if carried:
        carry_in, rest = rest[:2], rest[2:]
    outs, rest = rest[: 4 if pairs else 1], rest[4 if pairs else 1 :]
    totals_out, scratch = rest[: 4 if pairs else 2], rest[4 if pairs else 2 :]
    weights, made, totals, product, narrowed, sems = scratch
    step, last = pl.program_id(0), pl.num_programs(0) - 1
    tokens, width = normed.shape
    shard = shards.shape[2]
    own = tokens // 2
    loads = []
    if carried:
        loads = [pltpu.make_async_copy(carry_in[i], totals.at[i], sems.at[i]) for i in range(2)]
    if pairs:
        saves = [
            pltpu.make_async_copy(totals.at[i, pl.ds(0, own)], totals_out[i], sems.at[i])
            for i in range(2)
        ] + [
            pltpu.make_async_copy(narrowed.at[i], totals_out[2 + i], sems.at[2 + i])
            for i in range(2)
        ]
    else:
        saves = [pltpu.make_async_copy(totals.at[i], totals_out[i], sems.at[i]) for i in range(2)]

    @pl.when(step == 0)
    def _():
        for copy in loads:
            copy.start()
        if not carried:
            totals[...] = jnp.zeros_like(totals)

    for place in range(shards.shape[0]):
        for kind in range(3):
            weights[kind, place * shard : (place + 1) * shard] = shards[place, kind]

    for block in range(tokens // TOKEN_BLOCK):
        at = slice(block * TOKEN_BLOCK, (block + 1) * TOKEN_BLOCK)
        gate = wide_dot(normed[at], weights[0])
        up = wide_dot(normed[at], weights[1])
        grad = wide_dot(cotangent[at], weights[2])
        sigm = 0.5 + 0.5 * jnp.tanh(0.5 * gate)
        silu = gate * sigm
        made[0, at] = narrow(grad * up * (sigm + silu * (1.0 - sigm)))
        made[1, at] = narrow(grad * silu)
        made[2, at] = narrow(silu * up)

    @pl.when(step == 0)
    def _():
        for copy in loads:
            copy.wait()

    for block in range(tokens // TOKEN_BLOCK):
        at = slice(block * TOKEN_BLOCK, (block + 1) * TOKEN_BLOCK)
        totals[0, at] += wide_dot_t(made[2, at], weights[2])
        totals[1, at] += wide_dot_t(made[0, at], weights[0]) + wide_dot_t(
            made[1, at], weights[1]
        )

    @pl.when(step == last)
    def _():
        if pairs:
            narrowed[...] = narrow(totals[:, own:])
        for copy in saves:
            copy.start()

    for kind in range(3):
        left = cotangent_t if kind == 2 else normed_t
        made_grad = narrow(wide_dot(left[...], made[kind]))
        if pairs:
            product[kind] = made_grad.reshape(product.shape[1:])
        else:
            for place in range(shards.shape[0]):
                outs[0][place, kind] = made_grad[place * shard : (place + 1) * shard]

    if pairs:
        first_tiles = pairs

        @pl.when(step < first_tiles)
        def _():
            for kind in range(3):
                cut_first(product, kind, bits, outs[0], outs[1], kind)

        @pl.when(step >= first_tiles)
        def _():
            for kind in range(3):
                cut_second(product, kind, bits, outs[2], outs[3], kind)

    @pl.when(step == last)
    def _():
        for copy in saves:
            copy.wait()


def ffn_call(bits, rows, rows_t, shards, pairs=False, carry=()):
    tokens, width = rows[0].shape
    places, _, shard, units = shards.shape
    tiles = units // TILE
    whole = pl.BlockSpec((tokens, width), lambda i, b: (0, 0), pipeline_mode=pl.Buffered(1))
    whole_t = pl.BlockSpec((width, tokens), lambda i, b: (0, 0), pipeline_mode=pl.Buffered(1))
    natural = pl.BlockSpec((places, 3, shard, TILE), lambda i, b: (0, 0, 0, i))
    anywhere = pl.BlockSpec(memory_space=pl.ANY)
    own = tokens // 2
    shape = lambda *dims, dtype=jnp.bfloat16: jax.ShapeDtypeStruct(dims, dtype)
    if pairs:
        first_tiles = tiles // 2
        piece = (2, 4, 3, shard)
        first_spec = pl.BlockSpec(
            piece + (TILE,), lambda i, b: (0, 0, 0, 0, jnp.minimum(i, first_tiles - 1))
        )
        second_spec = pl.BlockSpec(
            piece + (TILE,), lambda i, b: (0, 0, 0, 0, jnp.maximum(i - first_tiles, 0))
        )
        out_specs = [first_spec] * 2 + [second_spec] * 2 + [anywhere] * 4
        first_shape = shape(*piece, first_tiles * TILE)
        second_shape = shape(*piece, units - first_tiles * TILE)
        out_shape = [first_shape] * 2 + [second_shape] * 2
        out_shape += [shape(own, width, dtype=jnp.float32)] * 2 + [shape(own, width)] * 2
    else:
        first_tiles = 0
        out_specs = [natural] + [anywhere] * 2
        out_shape = [shape(*shards.shape)] + [shape(tokens, width, dtype=jnp.float32)] * 2
    return pl.pallas_call(
        functools.partial(ffn_kernel, pairs=first_tiles, carried=bool(carry)),
        out_shape=out_shape,
        grid_spec=pltpu.PrefetchScalarGridSpec(
            num_scalar_prefetch=1,
            grid=(tiles,),
            in_specs=[whole] * 2 + [whole_t] * 2 + [natural] + [anywhere] * len(carry),
            out_specs=out_specs,
            scratch_shapes=[
                pltpu.VMEM((3, width, TILE), jnp.bfloat16),
                pltpu.VMEM((3, tokens, TILE), jnp.bfloat16),
                pltpu.VMEM((2, tokens, width), jnp.float32),
                pltpu.VMEM((3, 4, 2, 2, shard, TILE), jnp.bfloat16),
                pltpu.VMEM((2, own, width) if pairs else (2, 16, 128), jnp.bfloat16),
                pltpu.SemaphoreType.DMA((4,)),
            ],
        ),
        compiler_params=pltpu.CompilerParams(
            dimension_semantics=("arbitrary",), vmem_limit_bytes=VMEM_LIMIT
        ),
        cost_estimate=work(tokens, width, 9 * units, 40 * tokens * width),
        name="ffn",
    )(bits, *rows, *rows_t, shards, *carry)


def earlier(values, steps):
    row = lax.broadcasted_iota(jnp.int32, values.shape, 0)
    return jnp.where(row >= steps, pltpu.roll(values, steps, 0), 0.0)


def later(values, steps):
    rows = values.shape[0]
    row = lax.broadcasted_iota(jnp.int32, values.shape, 0)
    return jnp.where(row < rows - steps, pltpu.roll(values, rows - steps, 0), 0.0)


def convolve(mixed, taps):
    return taps[0:1] * earlier(mixed, 2) + taps[1:2] * earlier(mixed, 1) + taps[2:3] * mixed


def mixer_kernel(
    bits, normed, taps, first_own, first_other, second_own, second_other,
    saved, kept_weights, own_out, other_out, weights, total,
):
    step, last = pl.program_id(0), pl.num_programs(0) - 1
    place_pieces(weights, 4, bits, (first_own, first_other), (second_own, second_other), 2)
    width = normed.shape[1]
    for kind in range(4):
        kept_weights[kind] = weights[kind].reshape(width, TILE)

    @pl.when(step == 0)
    def _():
        total[...] = jnp.zeros_like(total)

    tap_rows = taps[...].astype(jnp.float32)
    for block in range(normed.shape[0] // LEN):
        at = slice(block * LEN, (block + 1) * LEN)
        b_rows = wide_dot(normed[at], kept_weights[0])
        x_rows = wide_dot(normed[at], kept_weights[2])
        c_rows = wide_dot(normed[at], kept_weights[1])
        saved[0, at], saved[1, at], saved[2, at] = b_rows, c_rows, x_rows
        gated = narrow(c_rows * convolve(b_rows * x_rows, tap_rows))
        total[at] += wide_dot_t(gated, kept_weights[3])

    @pl.when(step == last)
    def _():
        own = total.shape[0] // 2
        own_out[...] = total[:own]
        other_out[...] = narrow(total[own:])


def mixer_call(bits, normed, taps, first, second):
    tokens, width = normed.shape
    shard, channels = first[0].shape[3:]
    own = tokens // 2
    still = lambda *dims: pl.BlockSpec(dims, lambda i, b: (0,) * len(dims), pipeline_mode=pl.Buffered(1))
    piece = pl.BlockSpec((2, 4, 2, shard, TILE), lambda i, b: (0, 0, 0, 0, i))
    return pl.pallas_call(
        mixer_kernel,
        out_shape=[
            jax.ShapeDtypeStruct((3, tokens, channels), jnp.float32),
            jax.ShapeDtypeStruct((4, width, channels), jnp.bfloat16),
            jax.ShapeDtypeStruct((own, width), jnp.float32),
            jax.ShapeDtypeStruct((own, width), jnp.bfloat16),
        ],
        grid_spec=pltpu.PrefetchScalarGridSpec(
            num_scalar_prefetch=1,
            grid=(channels // TILE,),
            in_specs=[still(tokens, width), pl.BlockSpec((3, TILE), lambda i, b: (0, i))]
            + [piece] * 4,
            out_specs=[
                pl.BlockSpec((3, tokens, TILE), lambda i, b: (0, 0, i)),
                pl.BlockSpec((4, width, TILE), lambda i, b: (0, 0, i)),
                pl.BlockSpec((own, width), lambda i, b: (0, 0)),
                pl.BlockSpec((own, width), lambda i, b: (0, 0)),
            ],
            scratch_shapes=[
                pltpu.VMEM((4, 4, 2, 2, shard, TILE), jnp.bfloat16),
                pltpu.VMEM((tokens, width), jnp.float32),
            ],
        ),
        compiler_params=pltpu.CompilerParams(
            dimension_semantics=("arbitrary",), vmem_limit_bytes=VMEM_LIMIT
        ),
        cost_estimate=work(tokens, width, 4 * channels, 40 * tokens * width),
        name="mixer",
    )(bits, normed, taps, *first, *second)


def mixer_back_kernel(
    bits, grads, grads_t, normed_t, taps, saved, weights,
    first_send, first_keep, second_send, second_keep, own_out, other_out, taps_grad,
    made, product, total,
):
    step, last = pl.program_id(0), pl.num_programs(0) - 1

    @pl.when(step == 0)
    def _():
        total[...] = jnp.zeros_like(total)

    tap_rows = taps[...].astype(jnp.float32)
    tap_sums = [jnp.zeros((1, TILE), jnp.float32) for _ in range(3)]
    for block in range(grads.shape[0] // LEN):
        at = slice(block * LEN, (block + 1) * LEN)
        grad_gated = wide_dot(grads[at], weights[3])
        b_rows, c_rows, x_rows = saved[0, at], saved[1, at], saved[2, at]
        mixed = b_rows * x_rows
        shifted = [earlier(mixed, 2), earlier(mixed, 1), mixed]
        convolved = sum(tap_rows[k : k + 1] * shifted[k] for k in range(3))
        grad_conv = grad_gated * c_rows
        tap_sums = [
            tap_sums[k] + jnp.sum(grad_conv * shifted[k], axis=0, keepdims=True) for k in range(3)
        ]
        grad_mixed = (
            tap_rows[0:1] * later(grad_conv, 2)
            + tap_rows[1:2] * later(grad_conv, 1)
            + tap_rows[2:3] * grad_conv
        )
        made[0, at] = narrow(grad_mixed * x_rows)
        made[1, at] = narrow(grad_gated * convolved)
        made[2, at] = narrow(grad_mixed * b_rows)
        made[3, at] = narrow(c_rows * convolved)
    for k in range(3):
        taps_grad[k : k + 1] = tap_sums[k]
    for block in range(grads.shape[0] // TOKEN_BLOCK):
        at = slice(block * TOKEN_BLOCK, (block + 1) * TOKEN_BLOCK)
        total[at] += (
            wide_dot_t(made[0, at], weights[0])
            + wide_dot_t(made[1, at], weights[1])
            + wide_dot_t(made[2, at], weights[2])
        )

    @pl.when(step == last)
    def _():
        own = total.shape[0] // 2
        own_out[...] = total[:own]
        other_out[...] = narrow(total[own:])

    for kind in range(4):
        left = grads_t if kind == 3 else normed_t
        product[kind] = narrow(wide_dot(left[...], made[kind])).reshape(product.shape[1:])
        if kind < 2:
            cut_first(product, kind, bits, first_send, first_keep, kind)
        else:
            cut_second(product, kind, bits, second_send, second_keep, kind - 2)


def mixer_back_call(bits, grads, grads_t, normed_t, taps, saved, weights):
    tokens, width = grads.shape
    channels = taps.shape[1]
    shard = width // 16
    own = tokens // 2
    still = lambda *dims: pl.BlockSpec(dims, lambda i, b: (0,) * len(dims), pipeline_mode=pl.Buffered(1))
    piece = pl.BlockSpec((2, 4, 2, shard, TILE), lambda i, b: (0, 0, 0, 0, i))
    return pl.pallas_call(
        mixer_back_kernel,
        out_shape=[jax.ShapeDtypeStruct((2, 4, 2, shard, channels), jnp.bfloat16)] * 4
        + [
            jax.ShapeDtypeStruct((own, width), jnp.float32),
            jax.ShapeDtypeStruct((own, width), jnp.bfloat16),
            jax.ShapeDtypeStruct((3, channels), jnp.float32),
        ],
        grid_spec=pltpu.PrefetchScalarGridSpec(
            num_scalar_prefetch=1,
            grid=(channels // TILE,),
            in_specs=[
                still(tokens, width),
                still(width, tokens),
                still(width, tokens),
                pl.BlockSpec((3, TILE), lambda i, b: (0, i)),
                pl.BlockSpec((3, tokens, TILE), lambda i, b: (0, 0, i)),
                pl.BlockSpec((4, width, TILE), lambda i, b: (0, 0, i)),
            ],
            out_specs=[piece] * 4
            + [
                pl.BlockSpec((own, width), lambda i, b: (0, 0)),
                pl.BlockSpec((own, width), lambda i, b: (0, 0)),
                pl.BlockSpec((3, TILE), lambda i, b: (0, i)),
            ],
            scratch_shapes=[
                pltpu.VMEM((4, tokens, TILE), jnp.bfloat16),
                pltpu.VMEM((4, 4, 2, 2, shard, TILE), jnp.bfloat16),
                pltpu.VMEM((tokens, width), jnp.float32),
            ],
        ),
        compiler_params=pltpu.CompilerParams(
            dimension_semantics=("arbitrary",), vmem_limit_bytes=VMEM_LIMIT
        ),
        cost_estimate=work(tokens, width, 9 * channels, 40 * tokens * width),
        name="mixer_back",
    )(bits, grads, grads_t, normed_t, taps, saved, weights)


def per_device_pairs(
    tokens,
    norm_gain1,
    in_weight,
    conv_kernel,
    out_weight,
    norm_gain2,
    gate_up_weight,
    down_weight,
    out_grad,
):
    rows, width = tokens.shape
    split = down_weight.shape[1] // (2 * TILE) * TILE
    collect = lambda values: both_call(values, exchange(values))
    bits = jnp.stack(place_bits()[:0:-1]).astype(jnp.int32)
    gain1, gain2 = norm_gain1[None], norm_gain2[None]
    wide_rows = ((rows, width), jnp.float32)
    narrow_rows = ((rows, width), jnp.bfloat16)
    gain_row = ((1, width), jnp.float32)

    small = jnp.concatenate([jnp.transpose(in_weight, (1, 0, 2)), out_weight[None]], 0)
    big = jnp.concatenate([jnp.transpose(gate_up_weight, (1, 0, 2)), down_weight[None]], 0)
    big1 = lax.all_gather(big[..., :split], "dp", axis=0)
    big2 = lax.all_gather(big[..., split:], "dp", axis=0)

    near = line_near(small)
    (normed1,) = row_call(norm_kernel, "norm", (tokens, gain1), (narrow_rows,))
    group_n1, normed1_t = collect(normed1)
    lines = line_far(near, line_middle(near))
    lines, group_n1 = tie(lines, group_n1)
    s_first, s_second = gather_pair(lines[:, :2], 2), gather_pair(lines[:, 2:], 1)
    group_grad, cotangent_t = collect(out_grad)
    s_first, s_second, group_grad, cotangent_t, normed1_t = tie(
        s_first, s_second, group_grad, cotangent_t, normed1_t
    )
    s_first, s_second = (s_first, across(s_first, 1)), (s_second, across(s_second, 2))
    saved, mixer_weights, own, other = mixer_call(bits, group_n1, conv_kernel, s_first, s_second)
    middle, normed2 = row_call(
        middle_kernel, "middle", (tokens, own, exchange(other), gain2), (wide_rows, narrow_rows)
    )
    group_n2, normed2_t = collect(normed2)
    rows_both, rows_t = (group_n2, group_grad), (normed2_t, cotangent_t)

    grads1, *carry = ffn_call(bits, rows_both, rows_t, big1)
    grads1 = lax.psum_scatter(grads1, "dp", scatter_dimension=0)
    send2, keep2, send2b, keep2b, forward, backward, forward_other, backward_other = ffn_call(
        bits, rows_both, rows_t, big2, True, tuple(carry)
    )
    backward_other = exchange(backward_other)
    took2, took2b = across(send2, 1), across(send2b, 2)
    grad_middle, narrowed, gain_two_grad = row_call(
        middle_back_kernel,
        "middle_back",
        (backward, backward_other, middle, gain2, out_grad),
        (wide_rows, narrow_rows, gain_row),
    )
    group_gm, grads_t = collect(narrowed)
    s_send, s_keep, s_sendb, s_keepb, own, other, kernel_grad = mixer_back_call(
        bits, group_gm, grads_t, normed1_t, conv_kernel, saved, mixer_weights
    )
    took2, took2b, s_send, s_keep, s_sendb, s_keepb, own, other, kernel_grad = tie(
        took2, took2b, s_send, s_keep, s_sendb, s_keepb, own, other, kernel_grad
    )

    first2, second2 = narrow(add_wide(keep2, took2)), narrow(add_wide(keep2b, took2b))
    first2, second2 = reduce_pair(first2, 2), reduce_pair(second2, 1)
    s_first = narrow(add_wide(s_keep, across(s_send, 1)))
    s_second = narrow(add_wide(s_keepb, across(s_sendb, 2)))
    input_grad, gain_one_grad = row_call(
        input_back_kernel,
        "input_back",
        (own, exchange(other), tokens, gain1, grad_middle),
        (wide_rows, gain_row),
    )
    summed = jnp.concatenate([gain_one_grad, gain_two_grad, kernel_grad.reshape(1, -1)], 1)
    first2, second2, s_first, s_second, summed = tie(first2, second2, s_first, s_second, summed)

    s_first, s_second = reduce_pair(s_first, 2), reduce_pair(s_second, 1)
    mine2, theirs2 = reduce_far(jnp.concatenate([first2, second2], -1))
    result = narrow(middle + (forward + exchange(forward_other).astype(jnp.float32)))
    summed = summed + across(summed, 1)
    summed = summed + across(summed, 2)
    s_first, s_second, mine2, theirs2, summed, result = tie(
        s_first, s_second, mine2, theirs2, summed, result
    )

    mine_s, theirs_s = reduce_far(jnp.concatenate([s_first, s_second], 1))
    mine2 = reduce_middle(mine2, theirs2)
    summed = summed + across(summed, 4)
    mine_s, theirs_s, mine2, summed = tie(mine_s, theirs_s, mine2, summed)
    grads2 = reduce_near(mine2)
    mine_s = reduce_middle(mine_s, theirs_s)
    summed = summed + across(summed, 8)
    mine_s, grads2, summed = tie(mine_s, grads2, summed)
    small_grads = reduce_near(mine_s)
    gains = summed[0, : 2 * width]
    gains = gains + exchange(gains)
    big_grads = jnp.concatenate([grads1.astype(jnp.float32), grads2], -1)
    return (
        result,
        input_grad,
        gains[:width],
        jnp.transpose(small_grads[:3], (1, 0, 2)),
        summed[0, 2 * width :].reshape(kernel_grad.shape),
        small_grads[3],
        gains[width:],
        jnp.transpose(big_grads[:2], (1, 0, 2)),
        big_grads[2],
    )


def solution(mesh):
    paired = mesh.shape["dp"] == 16 and mesh.shape["tensor"] == 2
    return jax.shard_map(
        per_device_pairs if paired else per_device,
        mesh=mesh,
        in_specs=(
            P(("dp", "tensor"), None),
            P(),
            P("dp", None, "tensor"),
            P(None, "tensor"),
            P("dp", "tensor"),
            P(),
            P("dp", None, "tensor"),
            P("dp", "tensor"),
            P(("dp", "tensor"), None),
        ),
        out_specs=(
            P(("dp", "tensor"), None),
            P(("dp", "tensor"), None),
            P(),
            P("dp", None, "tensor"),
            P(None, "tensor"),
            P("dp", "tensor"),
            P(),
            P("dp", None, "tensor"),
            P("dp", "tensor"),
        ),
        check_vma=False,
    )
```

```python
import functools

import jax
import jax.numpy as jnp
from jax import lax
from jax.experimental import pallas as pl
from jax.experimental.pallas import tpu as pltpu
from jax.sharding import PartitionSpec as P

LEN = 1024


eps = 1e-05


def rms_forward(stream, norm_gain):
    inverse = lax.rsqrt(jnp.mean(stream * stream, axis=-1, keepdims=True) + eps)
    unit_rows = stream * inverse
    return (unit_rows * norm_gain, unit_rows, inverse)


def rms_backward(grad_normed, unit_rows, inverse, norm_gain):
    gain_grad = jnp.sum(grad_normed * unit_rows, axis=0)
    grad_unit = grad_normed * norm_gain
    along = jnp.mean(grad_unit * unit_rows, axis=-1, keepdims=True)
    return (inverse * (grad_unit - unit_rows * along), gain_grad)


def causal_conv(values, kernel):
    channels = values.shape[-1]
    blocks = values.reshape(-1, LEN, channels)
    padded = jnp.pad(blocks, ((0, 0), (2, 0), (0, 0)))
    summed = (
        kernel[0] * padded[:, 0:LEN]
        + kernel[1] * padded[:, 1 : LEN + 1]
        + kernel[2] * padded[:, 2 : LEN + 2]
    )
    return summed.reshape(values.shape)


def conv_backward(grad_out, values, kernel):
    channels = values.shape[-1]
    grad_blocks = grad_out.reshape(-1, LEN, channels)
    padded = jnp.pad(values.reshape(-1, LEN, channels), ((0, 0), (2, 0), (0, 0)))
    kernel_grad = jnp.stack(
        [
            jnp.sum(grad_blocks * padded[:, 0:LEN], axis=(0, 1)),
            jnp.sum(grad_blocks * padded[:, 1 : LEN + 1], axis=(0, 1)),
            jnp.sum(grad_blocks * padded[:, 2 : LEN + 2], axis=(0, 1)),
        ]
    )
    later = jnp.pad(grad_blocks, ((0, 0), (0, 2), (0, 0)))
    grad_values = (
        kernel[0] * later[:, 2 : LEN + 2]
        + kernel[1] * later[:, 1 : LEN + 1]
        + kernel[2] * later[:, 0:LEN]
    )
    return (grad_values.reshape(values.shape), kernel_grad)


def mixer_forward(normed_rows, in_w, kernel):
    projected = jnp.einsum("td,dkc->tkc", normed_rows, in_w, preferred_element_type=jnp.float32)
    mixed_in = projected[:, 0] * projected[:, 2]
    convolved = causal_conv(mixed_in, kernel)
    gated = (projected[:, 1] * convolved).astype(jnp.bfloat16)
    return (projected, mixed_in, convolved, gated)


def mixer_backward(grad_gated, projected, mixed_in, convolved, kernel):
    grad_c = grad_gated * convolved
    grad_conv = grad_gated * projected[:, 1]
    grad_mixed, kernel_grad = conv_backward(grad_conv, mixed_in, kernel)
    grad_stack = jnp.stack(
        [grad_mixed * projected[:, 2], grad_c, grad_mixed * projected[:, 0]], axis=1
    )
    return (grad_stack.astype(jnp.bfloat16), kernel_grad)


def ffn_forward(normed_rows, gate_up_w):
    gate_up = jnp.einsum("td,dkf->tkf", normed_rows, gate_up_w, preferred_element_type=jnp.float32)
    hidden = (jax.nn.silu(gate_up[:, 0]) * gate_up[:, 1]).astype(jnp.bfloat16)
    return (gate_up, hidden)


def ffn_backward(grad_hidden, gate_up):
    gate = gate_up[:, 0]
    sigm = jax.nn.sigmoid(gate)
    grad_up = grad_hidden * gate * sigm
    grad_gate = grad_hidden * gate_up[:, 1] * sigm * (1.0 + gate * (1.0 - sigm))
    return jnp.stack([grad_gate, grad_up], axis=1).astype(jnp.bfloat16)


def run_layer(
    tokens,
    out_grad,
    gain_one,
    gain_two,
    in_w,
    kernel_b,
    out_w,
    gate_up_w,
    down_w,
    mixer_movers,
    ffn_movers,
):
    collect_first, reduce_first, collect_grad1, reduce_back1 = mixer_movers
    collect_second, reduce_second, reduce_back2 = ffn_movers
    own_rows = tokens.shape[0]
    kernel = kernel_b.astype(jnp.float32)
    stream = tokens.astype(jnp.float32)
    normed1, unit1, inverse1 = rms_forward(stream, gain_one)
    group_n1 = collect_first(normed1.astype(jnp.bfloat16))
    projected, mixed_in, convolved, gated = mixer_forward(group_n1, in_w, kernel)

    def mix_term(first_row, row_count):
        return jnp.einsum("tc,jc->tj", gated, out_w, preferred_element_type=jnp.float32)

    middle = stream + reduce_first(mix_term, own_rows)
    normed2, unit2, inverse2 = rms_forward(middle, gain_two)
    group_n2, group_grad = collect_second((normed2.astype(jnp.bfloat16), out_grad))
    gate_up, hidden = ffn_forward(group_n2, gate_up_w)

    def ffn_term(first_row, row_count):
        return jnp.einsum("tf,jf->tj", hidden, down_w, preferred_element_type=jnp.float32)

    result = (middle + reduce_second(ffn_term, own_rows)).astype(jnp.bfloat16)
    grad_hidden = jnp.dot(group_grad, down_w, preferred_element_type=jnp.float32)
    down_grad_w = jnp.einsum("tj,tf->jf", group_grad, hidden, preferred_element_type=jnp.float32)
    grad_gate_up = ffn_backward(grad_hidden, gate_up)
    gate_up_grad_w = jnp.einsum(
        "td,tkf->dkf", group_n2, grad_gate_up, preferred_element_type=jnp.float32
    )

    def ffn_back_term(first_row, row_count):
        return jnp.einsum(
            "tkf,dkf->td", grad_gate_up, gate_up_w, preferred_element_type=jnp.float32
        )

    grad_normed2 = reduce_back2(ffn_back_term, own_rows)
    grad_rms2, gain_two_grad = rms_backward(grad_normed2, unit2, inverse2, gain_two)
    grad_middle = out_grad.astype(jnp.float32) + grad_rms2
    group_gm = collect_grad1(grad_middle.astype(jnp.bfloat16))
    out_grad_w = jnp.einsum("tj,tc->jc", group_gm, gated, preferred_element_type=jnp.float32)
    grad_gated = jnp.einsum("tj,jc->tc", group_gm, out_w, preferred_element_type=jnp.float32)
    grad_projected, kernel_grad = mixer_backward(grad_gated, projected, mixed_in, convolved, kernel)
    in_grad_w = jnp.einsum(
        "td,tkc->dkc", group_n1, grad_projected, preferred_element_type=jnp.float32
    )

    def mixer_back_term(first_row, row_count):
        return jnp.einsum("tkc,dkc->td", grad_projected, in_w, preferred_element_type=jnp.float32)

    grad_normed1 = reduce_back1(mixer_back_term, own_rows)
    grad_rms1, gain_one_grad = rms_backward(grad_normed1, unit1, inverse1, gain_one)
    input_grad = grad_middle + grad_rms1
    return (
        result,
        input_grad,
        (gain_one_grad, gain_two_grad),
        (in_grad_w, out_grad_w),
        (gate_up_grad_w, down_grad_w),
        kernel_grad,
    )


def per_device(
    tokens,
    norm_gain1,
    in_weight,
    conv_kernel,
    out_weight,
    norm_gain2,
    gate_up_weight,
    down_weight,
    out_grad,
):
    channels = in_weight.shape[2]
    model_width = tokens.shape[1]
    in_part, out_part, gate_up_part, down_part = (
        lax.all_gather(in_weight, "dp", axis=0, tiled=True),
        lax.all_gather(out_weight, "dp", axis=0, tiled=True),
        lax.all_gather(gate_up_weight, "dp", axis=0, tiled=True),
        lax.all_gather(down_weight, "dp", axis=0, tiled=True),
    )
    in_use, out_use, kernel_use = (in_part, out_part, conv_kernel)

    def collect_first(values):
        return lax.all_gather(values, "tensor", axis=0, tiled=True)

    def reduce_first(term_fn, row_count):
        return lax.psum_scatter(
            term_fn(jnp.int32(0), lax.axis_size("tensor") * row_count),
            "tensor",
            scatter_dimension=0,
            tiled=True,
        )

    def collect_grad1(values):
        return lax.all_gather(values, "tensor", axis=0, tiled=True)

    def reduce_back1(term_fn, row_count):
        return lax.psum_scatter(
            term_fn(jnp.int32(0), lax.axis_size("tensor") * row_count),
            "tensor",
            scatter_dimension=0,
            tiled=True,
        )

    mixer_movers = (collect_first, reduce_first, collect_grad1, reduce_back1)
    gate_up_use, down_use = (gate_up_part, down_part)

    def collect_second(values):
        return (
            lax.all_gather(values[0], "tensor", axis=0, tiled=True),
            lax.all_gather(values[1], "tensor", axis=0, tiled=True),
        )

    def reduce_second(term_fn, row_count):
        return lax.psum_scatter(
            term_fn(jnp.int32(0), lax.axis_size("tensor") * row_count),
            "tensor",
            scatter_dimension=0,
            tiled=True,
        )

    def reduce_back2(term_fn, row_count):
        return lax.psum_scatter(
            term_fn(jnp.int32(0), lax.axis_size("tensor") * row_count),
            "tensor",
            scatter_dimension=0,
            tiled=True,
        )

    ffn_movers = (collect_second, reduce_second, reduce_back2)
    result, input_grad, gain_grads, mixer_grads, ffn_grads, kernel_grad = run_layer(
        tokens,
        out_grad,
        norm_gain1,
        norm_gain2,
        in_use,
        kernel_use,
        out_use,
        gate_up_use,
        down_use,
        mixer_movers,
        ffn_movers,
    )
    in_share, out_share = mixer_grads
    offset = lax.axis_index("tensor") * channels
    kernel_full = lax.dynamic_update_slice(
        jnp.zeros((3, model_width), jnp.float32), kernel_grad, (jnp.int32(0), offset)
    )
    gate_up_share, down_share = ffn_grads
    in_final, out_final, gate_up_final, down_final = (
        lax.psum_scatter(in_share, "dp", scatter_dimension=0, tiled=True),
        lax.psum_scatter(out_share, "dp", scatter_dimension=0, tiled=True),
        lax.psum_scatter(gate_up_share, "dp", scatter_dimension=0, tiled=True),
        lax.psum_scatter(down_share, "dp", scatter_dimension=0, tiled=True),
    )
    gain_one_sum, gain_two_sum, kernel_sum = lax.psum(
        (gain_grads[0], gain_grads[1], kernel_full), ("dp", "tensor")
    )
    conv_share = lax.dynamic_slice_in_dim(
        kernel_sum, lax.axis_index("tensor") * channels, channels, 1
    )
    return (
        result,
        input_grad,
        gain_one_sum,
        in_final,
        conv_share,
        out_final,
        gain_two_sum,
        gate_up_final,
        down_final,
    )


def exchange(values):
    return lax.ppermute(values, "tensor", [(0, 1), (1, 0)])


def across(values, bit):
    return lax.ppermute(values, "dp", [(place, place ^ bit) for place in range(16)])


def between(values, steps):
    pairs = [
        (place, place + 4 * shift)
        for level, shift in steps
        for place in range(4 * level, 4 * level + 4)
    ]
    return lax.ppermute(values, "dp", pairs)


def place_bits():
    place = lax.axis_index("dp")
    return place // 4, (place // 2) % 2, place % 2


def in_order(own_bit, own, other):
    return jnp.where(
        own_bit == 0, jnp.concatenate([own, other], 0), jnp.concatenate([other, own], 0)
    )


def tie(*values):
    return lax.optimization_barrier(values)


def add_wide(first, second):
    return first.astype(jnp.float32) + second.astype(jnp.float32)


def narrow(values):
    return values.astype(jnp.bfloat16)


def gather_direct(values):
    ups = [between(values, [(z, s) for z in range(4 - s)]) for s in (1, 2, 3)]
    downs = [between(values, [(z, -s) for z in range(s, 4)]) for s in (1, 2, 3)]
    line = jnp.stack(ups[::-1] + [values] + downs)
    return lax.dynamic_slice_in_dim(line, 3 - place_bits()[0], 4, 0)


def line_near(values):
    return in_order(place_bits()[0] % 2, values[None], across(values, 4)[None])


def line_middle(near):
    return between(near, [(1, 1), (2, -1)])


def line_far(near, middle):
    level = place_bits()[0]
    outer = between(middle, [(1, -1), (2, 1)])
    far = jnp.where((level == 1) | (level == 2), middle, outer)
    return in_order(level // 2, near, far)


def gather_pair(values, bit):
    own_bit = place_bits()[2 if bit == 1 else 1]
    return in_order(own_bit, values[None], across(values, bit)[None])


def pick(values, index):
    return lax.dynamic_index_in_dim(values, index, 0, keepdims=False)


def reduce_pair(values, bit):
    own_bit = place_bits()[2 if bit == 1 else 1]
    return narrow(add_wide(pick(values, own_bit), across(pick(values, 1 - own_bit), bit)))


def reduce_far(values):
    half = place_bits()[0] // 2
    mine = lax.dynamic_slice_in_dim(values, 2 * half, 2, 0)
    theirs = lax.dynamic_slice_in_dim(values, 2 - 2 * half, 2, 0)
    return mine, narrow(add_wide(theirs, between(theirs, [(0, 1), (3, -1)])))


def reduce_middle(mine, theirs):
    return narrow(add_wide(mine, between(theirs, [(1, 1), (2, -1)])))


def reduce_near(mine):
    bit = place_bits()[0] % 2
    return add_wide(pick(mine, bit), across(pick(mine, 1 - bit), 4))


def reduce_direct(values):
    level = place_bits()[0]
    total = pick(values, level).astype(jnp.float32)
    for s in (1, 2, 3):
        upper, lower = jnp.minimum(level + s, 3), jnp.maximum(level - s, 0)
        total = total + between(pick(values, upper), [(z, s) for z in range(4 - s)]).astype(
            jnp.float32
        )
        total = total + between(pick(values, lower), [(z, -s) for z in range(s, 4)]).astype(
            jnp.float32
        )
    return total


def sum_all(values):
    for bit in (1, 2, 4, 8):
        values = values + across(values, bit)
    return values


TILE = 256
TOKEN_BLOCK = 512
ROW_BLOCK = 256
VMEM_LIMIT = 60 * 1024 * 1024


def wide_dot(left, right):
    return jnp.dot(left, right, preferred_element_type=jnp.float32)


def wide_dot_t(left, right):
    return lax.dot_general(
        left, right, (((1,), (1,)), ((), ())), preferred_element_type=jnp.float32
    )


def unit_and_inverse(rows):
    inverse = lax.rsqrt(jnp.mean(rows * rows, axis=-1, keepdims=True) + eps)
    return rows * inverse, inverse


def norm_kernel(tokens, gain, normed):
    unit, _ = unit_and_inverse(tokens[...].astype(jnp.float32))
    normed[...] = narrow(unit * gain[...])


def middle_kernel(tokens, own, other, gain, middle, normed):
    rows = tokens[...].astype(jnp.float32) + (own[...] + other[...].astype(jnp.float32))
    middle[...] = rows
    unit, _ = unit_and_inverse(rows)
    normed[...] = narrow(unit * gain[...])


def norm_back(rows, grad, gain, gain_grad):
    unit, inverse = unit_and_inverse(rows)

    @pl.when(pl.program_id(0) == 0)
    def _():
        gain_grad[...] = jnp.zeros_like(gain_grad)

    gain_grad[...] += jnp.sum(grad * unit, axis=0, keepdims=True)
    grad_unit = grad * gain
    along = jnp.mean(grad_unit * unit, axis=-1, keepdims=True)
    return inverse * (grad_unit - unit * along)


def middle_back_kernel(own, other, middle, gain, out_grad, grad_middle, narrowed, gain_grad):
    grad = own[...] + other[...].astype(jnp.float32)
    total = out_grad[...].astype(jnp.float32) + norm_back(
        middle[...], grad, gain[...], gain_grad
    )
    grad_middle[...] = total
    narrowed[...] = narrow(total)


def input_back_kernel(own, other, tokens, gain, grad_middle, input_grad, gain_grad):
    grad = own[...] + other[...].astype(jnp.float32)
    input_grad[...] = grad_middle[...] + norm_back(
        tokens[...].astype(jnp.float32), grad, gain[...], gain_grad
    )


def work(matmul_rows, depth, columns, moved):
    return pl.CostEstimate(
        flops=2 * matmul_rows * depth * columns, transcendentals=0, bytes_accessed=moved
    )


def both_kernel(own, other, group, group_t):
    half = pl.num_programs(0) // 2

    @pl.when(pl.program_id(0) < half)
    def _():
        group[...] = own[...]
        group_t[...] = own[...].T

    @pl.when(pl.program_id(0) >= half)
    def _():
        group[...] = other[...]
        group_t[...] = other[...].T


def both_call(own, other):
    rows, width = own.shape
    steps = rows // ROW_BLOCK
    return pl.pallas_call(
        both_kernel,
        out_shape=[
            jax.ShapeDtypeStruct((2 * rows, width), own.dtype),
            jax.ShapeDtypeStruct((width, 2 * rows), own.dtype),
        ],
        grid=(2 * steps,),
        in_specs=[
            pl.BlockSpec((ROW_BLOCK, width), lambda i: (jnp.minimum(i, steps - 1), 0)),
            pl.BlockSpec((ROW_BLOCK, width), lambda i: (jnp.maximum(i - steps, 0), 0)),
        ],
        out_specs=[
            pl.BlockSpec((ROW_BLOCK, width), lambda i: (i, 0)),
            pl.BlockSpec((width, ROW_BLOCK), lambda i: (0, i)),
        ],
        compiler_params=pltpu.CompilerParams(vmem_limit_bytes=VMEM_LIMIT),
        cost_estimate=work(0, 0, 0, 12 * rows * width),
        name="both",
    )(own, other)


def row_call(kernel, name, args, outs):
    tokens = args[0].shape[0]
    spec = lambda shape: (
        pl.BlockSpec((ROW_BLOCK, shape[1]), lambda i: (i, 0))
        if shape[0] == tokens
        else pl.BlockSpec(shape, lambda i: (0, 0))
    )
    return pl.pallas_call(
        kernel,
        out_shape=[jax.ShapeDtypeStruct(*out) for out in outs],
        grid=(tokens // ROW_BLOCK,),
        in_specs=[spec(arg.shape) for arg in args],
        out_specs=[spec(out[0]) for out in outs],
        compiler_params=pltpu.CompilerParams(vmem_limit_bytes=VMEM_LIMIT),
        cost_estimate=work(0, 0, 0, 16 * tokens * args[0].shape[1]),
        name=name,
    )(*args)


def place_pieces(weights, kinds, bits, first, second, first_kinds):
    x_bit, y_bit = bits[0], bits[1]
    for side in range(2):
        for z in range(4):
            for kind in range(kinds):
                if kind < first_kinds:
                    weights[kind, z, side, pl.ds(x_bit, 1)] = first[0][side, z, kind][None]
                    weights[kind, z, side, pl.ds(1 - x_bit, 1)] = first[1][side, z, kind][None]
                else:
                    at = kind - first_kinds
                    weights[kind, z, pl.ds(y_bit, 1), side] = second[0][side, z, at][None]
                    weights[kind, z, pl.ds(1 - y_bit, 1), side] = second[1][side, z, at][None]


def cut_first(product, kind, bits, send, keep, at):
    for side in range(2):
        for z in range(4):
            keep[side, z, at] = product[kind, z, side, pl.ds(bits[0], 1)][0]
            send[side, z, at] = product[kind, z, side, pl.ds(1 - bits[0], 1)][0]


def cut_second(product, kind, bits, send, keep, at):
    for side in range(2):
        for z in range(4):
            keep[side, z, at] = product[kind, z, pl.ds(bits[1], 1), side][0]
            send[side, z, at] = product[kind, z, pl.ds(1 - bits[1], 1), side][0]


def ffn_kernel(
    bits, normed, cotangent, normed_t, cotangent_t, shards, *rest, pairs, carried, final
):
    if carried:
        carry_in, rest = rest[:2], rest[2:]
    outs, rest = rest[: 4 if pairs else 1], rest[4 if pairs else 1 :]
    totals_out, scratch = rest[: 4 if final else 2], rest[4 if final else 2 :]
    weights, made, totals, product, narrowed, sems = scratch
    step, last = pl.program_id(0), pl.num_programs(0) - 1
    tokens, width = normed.shape
    shard = shards.shape[2]
    own = tokens // 2
    loads = []
    if carried:
        loads = [pltpu.make_async_copy(carry_in[i], totals.at[i], sems.at[i]) for i in range(2)]
    if final:
        saves = [
            pltpu.make_async_copy(totals.at[i, pl.ds(0, own)], totals_out[i], sems.at[i])
            for i in range(2)
        ] + [
            pltpu.make_async_copy(narrowed.at[i], totals_out[2 + i], sems.at[2 + i])
            for i in range(2)
        ]
    else:
        saves = [pltpu.make_async_copy(totals.at[i], totals_out[i], sems.at[i]) for i in range(2)]

    @pl.when(step == 0)
    def _():
        for copy in loads:
            copy.start()
        if not carried:
            totals[...] = jnp.zeros_like(totals)

    for place in range(shards.shape[0]):
        for kind in range(3):
            weights[kind, place * shard : (place + 1) * shard] = shards[place, kind]

    for block in range(tokens // TOKEN_BLOCK):
        at = slice(block * TOKEN_BLOCK, (block + 1) * TOKEN_BLOCK)
        gate = wide_dot(normed[at], weights[0])
        up = wide_dot(normed[at], weights[1])
        grad = wide_dot(cotangent[at], weights[2])
        sigm = 0.5 + 0.5 * jnp.tanh(0.5 * gate)
        silu = gate * sigm
        made[0, at] = narrow(grad * up * (sigm + silu * (1.0 - sigm)))
        made[1, at] = narrow(grad * silu)
        made[2, at] = narrow(silu * up)

    @pl.when(step == 0)
    def _():
        for copy in loads:
            copy.wait()

    for block in range(tokens // TOKEN_BLOCK):
        at = slice(block * TOKEN_BLOCK, (block + 1) * TOKEN_BLOCK)
        totals[0, at] += wide_dot_t(made[2, at], weights[2])
        totals[1, at] += wide_dot_t(made[0, at], weights[0]) + wide_dot_t(
            made[1, at], weights[1]
        )

    @pl.when(step == last)
    def _():
        if final:
            narrowed[...] = narrow(totals[:, own:])
        for copy in saves:
            copy.start()

    for kind in range(3):
        left = cotangent_t if kind == 2 else normed_t
        made_grad = narrow(wide_dot(left[...], made[kind]))
        if pairs:
            product[kind] = made_grad.reshape(product.shape[1:])
        else:
            for place in range(shards.shape[0]):
                outs[0][place, kind] = made_grad[place * shard : (place + 1) * shard]

    if pairs:
        first_tiles = pairs

        @pl.when(step < first_tiles)
        def _():
            for kind in range(3):
                cut_first(product, kind, bits, outs[0], outs[1], kind)

        @pl.when(step >= first_tiles)
        def _():
            for kind in range(3):
                cut_second(product, kind, bits, outs[2], outs[3], kind)

    @pl.when(step == last)
    def _():
        for copy in saves:
            copy.wait()


def ffn_call(bits, rows, rows_t, shards, pairs, carry=()):
    tokens, width = rows[0].shape
    places, _, shard, units = shards.shape
    tiles = units // TILE
    whole = pl.BlockSpec((tokens, width), lambda i, b: (0, 0), pipeline_mode=pl.Buffered(1))
    whole_t = pl.BlockSpec((width, tokens), lambda i, b: (0, 0), pipeline_mode=pl.Buffered(1))
    natural = pl.BlockSpec((places, 3, shard, TILE), lambda i, b: (0, 0, 0, i))
    anywhere = pl.BlockSpec(memory_space=pl.ANY)
    own = tokens // 2
    shape = lambda *dims, dtype=jnp.bfloat16: jax.ShapeDtypeStruct(dims, dtype)
    if pairs:
        first_tiles = tiles // 2
        piece = (2, 4, 3, shard)
        first_spec = pl.BlockSpec(
            piece + (TILE,), lambda i, b: (0, 0, 0, 0, jnp.minimum(i, first_tiles - 1))
        )
        second_spec = pl.BlockSpec(
            piece + (TILE,), lambda i, b: (0, 0, 0, 0, jnp.maximum(i - first_tiles, 0))
        )
        out_specs = [first_spec] * 2 + [second_spec] * 2
        first_shape = shape(*piece, first_tiles * TILE)
        second_shape = shape(*piece, units - first_tiles * TILE)
        out_shape = [first_shape] * 2 + [second_shape] * 2
    else:
        first_tiles = 0
        out_specs = [natural]
        out_shape = [shape(*shards.shape)]
    final = bool(carry)
    if final:
        out_shape += [shape(own, width, dtype=jnp.float32)] * 2 + [shape(own, width)] * 2
    else:
        out_shape += [shape(tokens, width, dtype=jnp.float32)] * 2
    out_specs += [anywhere] * (4 if final else 2)
    return pl.pallas_call(
        functools.partial(ffn_kernel, pairs=first_tiles, carried=final, final=final),
        out_shape=out_shape,
        grid_spec=pltpu.PrefetchScalarGridSpec(
            num_scalar_prefetch=1,
            grid=(tiles,),
            in_specs=[whole] * 2 + [whole_t] * 2 + [natural] + [anywhere] * len(carry),
            out_specs=out_specs,
            scratch_shapes=[
                pltpu.VMEM((3, width, TILE), jnp.bfloat16),
                pltpu.VMEM((3, tokens, TILE), jnp.bfloat16),
                pltpu.VMEM((2, tokens, width), jnp.float32),
                pltpu.VMEM((3, 4, 2, 2, shard, TILE), jnp.bfloat16),
                pltpu.VMEM((2, own, width) if final else (2, 16, 128), jnp.bfloat16),
                pltpu.SemaphoreType.DMA((4,)),
            ],
        ),
        compiler_params=pltpu.CompilerParams(
            dimension_semantics=("arbitrary",), vmem_limit_bytes=VMEM_LIMIT
        ),
        cost_estimate=work(tokens, width, 9 * units, 40 * tokens * width),
        name="ffn",
    )(bits, *rows, *rows_t, shards, *carry)


def earlier(values, steps):
    row = lax.broadcasted_iota(jnp.int32, values.shape, 0)
    return jnp.where(row >= steps, pltpu.roll(values, steps, 0), 0.0)


def later(values, steps):
    rows = values.shape[0]
    row = lax.broadcasted_iota(jnp.int32, values.shape, 0)
    return jnp.where(row < rows - steps, pltpu.roll(values, rows - steps, 0), 0.0)


def convolve(mixed, taps):
    return taps[0:1] * earlier(mixed, 2) + taps[1:2] * earlier(mixed, 1) + taps[2:3] * mixed


def mixer_kernel(
    bits, normed, taps, first_own, first_other, second_own, second_other,
    saved, kept_weights, own_out, other_out, weights, total,
):
    step, last = pl.program_id(0), pl.num_programs(0) - 1
    place_pieces(weights, 4, bits, (first_own, first_other), (second_own, second_other), 2)
    width = normed.shape[1]
    for kind in range(4):
        kept_weights[kind] = weights[kind].reshape(width, TILE)

    @pl.when(step == 0)
    def _():
        total[...] = jnp.zeros_like(total)

    tap_rows = taps[...].astype(jnp.float32)
    for block in range(normed.shape[0] // LEN):
        at = slice(block * LEN, (block + 1) * LEN)
        b_rows = wide_dot(normed[at], kept_weights[0])
        x_rows = wide_dot(normed[at], kept_weights[2])
        c_rows = wide_dot(normed[at], kept_weights[1])
        saved[0, at], saved[1, at], saved[2, at] = b_rows, c_rows, x_rows
        gated = narrow(c_rows * convolve(b_rows * x_rows, tap_rows))
        total[at] += wide_dot_t(gated, kept_weights[3])

    @pl.when(step == last)
    def _():
        own = total.shape[0] // 2
        own_out[...] = total[:own]
        other_out[...] = narrow(total[own:])


def mixer_call(bits, normed, taps, first, second):
    tokens, width = normed.shape
    shard, channels = first[0].shape[3:]
    own = tokens // 2
    still = lambda *dims: pl.BlockSpec(dims, lambda i, b: (0,) * len(dims), pipeline_mode=pl.Buffered(1))
    piece = pl.BlockSpec((2, 4, 2, shard, TILE), lambda i, b: (0, 0, 0, 0, i))
    return pl.pallas_call(
        mixer_kernel,
        out_shape=[
            jax.ShapeDtypeStruct((3, tokens, channels), jnp.float32),
            jax.ShapeDtypeStruct((4, width, channels), jnp.bfloat16),
            jax.ShapeDtypeStruct((own, width), jnp.float32),
            jax.ShapeDtypeStruct((own, width), jnp.bfloat16),
        ],
        grid_spec=pltpu.PrefetchScalarGridSpec(
            num_scalar_prefetch=1,
            grid=(channels // TILE,),
            in_specs=[still(tokens, width), pl.BlockSpec((3, TILE), lambda i, b: (0, i))]
            + [piece] * 4,
            out_specs=[
                pl.BlockSpec((3, tokens, TILE), lambda i, b: (0, 0, i)),
                pl.BlockSpec((4, width, TILE), lambda i, b: (0, 0, i)),
                pl.BlockSpec((own, width), lambda i, b: (0, 0)),
                pl.BlockSpec((own, width), lambda i, b: (0, 0)),
            ],
            scratch_shapes=[
                pltpu.VMEM((4, 4, 2, 2, shard, TILE), jnp.bfloat16),
                pltpu.VMEM((tokens, width), jnp.float32),
            ],
        ),
        compiler_params=pltpu.CompilerParams(
            dimension_semantics=("arbitrary",), vmem_limit_bytes=VMEM_LIMIT
        ),
        cost_estimate=work(tokens, width, 4 * channels, 40 * tokens * width),
        name="mixer",
    )(bits, normed, taps, *first, *second)


def mixer_back_kernel(
    bits, grads, grads_t, normed_t, taps, saved, weights,
    first_send, first_keep, second_send, second_keep, own_out, other_out, taps_grad,
    made, product, total,
):
    step, last = pl.program_id(0), pl.num_programs(0) - 1

    @pl.when(step == 0)
    def _():
        total[...] = jnp.zeros_like(total)

    tap_rows = taps[...].astype(jnp.float32)
    tap_sums = [jnp.zeros((1, TILE), jnp.float32) for _ in range(3)]
    for block in range(grads.shape[0] // LEN):
        at = slice(block * LEN, (block + 1) * LEN)
        grad_gated = wide_dot(grads[at], weights[3])
        b_rows, c_rows, x_rows = saved[0, at], saved[1, at], saved[2, at]
        mixed = b_rows * x_rows
        shifted = [earlier(mixed, 2), earlier(mixed, 1), mixed]
        convolved = sum(tap_rows[k : k + 1] * shifted[k] for k in range(3))
        grad_conv = grad_gated * c_rows
        tap_sums = [
            tap_sums[k] + jnp.sum(grad_conv * shifted[k], axis=0, keepdims=True) for k in range(3)
        ]
        grad_mixed = (
            tap_rows[0:1] * later(grad_conv, 2)
            + tap_rows[1:2] * later(grad_conv, 1)
            + tap_rows[2:3] * grad_conv
        )
        made[0, at] = narrow(grad_mixed * x_rows)
        made[1, at] = narrow(grad_gated * convolved)
        made[2, at] = narrow(grad_mixed * b_rows)
        made[3, at] = narrow(c_rows * convolved)
    for k in range(3):
        taps_grad[k : k + 1] = tap_sums[k]
    for block in range(grads.shape[0] // TOKEN_BLOCK):
        at = slice(block * TOKEN_BLOCK, (block + 1) * TOKEN_BLOCK)
        total[at] += (
            wide_dot_t(made[0, at], weights[0])
            + wide_dot_t(made[1, at], weights[1])
            + wide_dot_t(made[2, at], weights[2])
        )

    @pl.when(step == last)
    def _():
        own = total.shape[0] // 2
        own_out[...] = total[:own]
        other_out[...] = narrow(total[own:])

    for kind in range(4):
        left = grads_t if kind == 3 else normed_t
        product[kind] = narrow(wide_dot(left[...], made[kind])).reshape(product.shape[1:])
        if kind < 2:
            cut_first(product, kind, bits, first_send, first_keep, kind)
        else:
            cut_second(product, kind, bits, second_send, second_keep, kind - 2)


def mixer_back_call(bits, grads, grads_t, normed_t, taps, saved, weights):
    tokens, width = grads.shape
    channels = taps.shape[1]
    shard = width // 16
    own = tokens // 2
    still = lambda *dims: pl.BlockSpec(dims, lambda i, b: (0,) * len(dims), pipeline_mode=pl.Buffered(1))
    piece = pl.BlockSpec((2, 4, 2, shard, TILE), lambda i, b: (0, 0, 0, 0, i))
    return pl.pallas_call(
        mixer_back_kernel,
        out_shape=[jax.ShapeDtypeStruct((2, 4, 2, shard, channels), jnp.bfloat16)] * 4
        + [
            jax.ShapeDtypeStruct((own, width), jnp.float32),
            jax.ShapeDtypeStruct((own, width), jnp.bfloat16),
            jax.ShapeDtypeStruct((3, channels), jnp.float32),
        ],
        grid_spec=pltpu.PrefetchScalarGridSpec(
            num_scalar_prefetch=1,
            grid=(channels // TILE,),
            in_specs=[
                still(tokens, width),
                still(width, tokens),
                still(width, tokens),
                pl.BlockSpec((3, TILE), lambda i, b: (0, i)),
                pl.BlockSpec((3, tokens, TILE), lambda i, b: (0, 0, i)),
                pl.BlockSpec((4, width, TILE), lambda i, b: (0, 0, i)),
            ],
            out_specs=[piece] * 4
            + [
                pl.BlockSpec((own, width), lambda i, b: (0, 0)),
                pl.BlockSpec((own, width), lambda i, b: (0, 0)),
                pl.BlockSpec((3, TILE), lambda i, b: (0, i)),
            ],
            scratch_shapes=[
                pltpu.VMEM((4, tokens, TILE), jnp.bfloat16),
                pltpu.VMEM((4, 4, 2, 2, shard, TILE), jnp.bfloat16),
                pltpu.VMEM((tokens, width), jnp.float32),
            ],
        ),
        compiler_params=pltpu.CompilerParams(
            dimension_semantics=("arbitrary",), vmem_limit_bytes=VMEM_LIMIT
        ),
        cost_estimate=work(tokens, width, 9 * channels, 40 * tokens * width),
        name="mixer_back",
    )(bits, grads, grads_t, normed_t, taps, saved, weights)


def per_device_pairs(
    tokens,
    norm_gain1,
    in_weight,
    conv_kernel,
    out_weight,
    norm_gain2,
    gate_up_weight,
    down_weight,
    out_grad,
):
    rows, width = tokens.shape
    split = (down_weight.shape[1] // TILE + 1) // 2 * TILE
    collect = lambda values: both_call(values, exchange(values))
    bits = jnp.stack(place_bits()[:0:-1]).astype(jnp.int32)
    gain1, gain2 = norm_gain1[None], norm_gain2[None]
    wide_rows = ((rows, width), jnp.float32)
    narrow_rows = ((rows, width), jnp.bfloat16)
    gain_row = ((1, width), jnp.float32)

    small = jnp.concatenate([jnp.transpose(in_weight, (1, 0, 2)), out_weight[None]], 0)
    big = jnp.concatenate([jnp.transpose(gate_up_weight, (1, 0, 2)), down_weight[None]], 0)
    big1 = lax.all_gather(big[..., :split], "dp", axis=0)
    big2 = lax.all_gather(big[..., split:], "dp", axis=0)
    near = line_near(small)
    (normed1,) = row_call(norm_kernel, "norm", (tokens, gain1), (narrow_rows,))
    lines = line_far(near, line_middle(near))
    normed1_other, out_grad_other = exchange(normed1), exchange(out_grad)
    s_first, s_second = gather_pair(lines[:, :2], 2), gather_pair(lines[:, 2:], 1)
    s_first, s_second, normed1_other, out_grad_other = tie(
        s_first, s_second, normed1_other, out_grad_other
    )
    s_other, s_otherb = across(s_first, 1), across(s_second, 2)
    group_n1, normed1_t = both_call(normed1, normed1_other)
    group_grad, cotangent_t = both_call(out_grad, out_grad_other)
    s_other, s_otherb, group_n1, normed1_t, group_grad, cotangent_t = tie(
        s_other, s_otherb, group_n1, normed1_t, group_grad, cotangent_t
    )
    s_first, s_second = (s_first, s_other), (s_second, s_otherb)
    saved, mixer_weights, own, other = mixer_call(bits, group_n1, conv_kernel, s_first, s_second)
    middle, normed2 = row_call(
        middle_kernel, "middle", (tokens, own, exchange(other), gain2), (wide_rows, narrow_rows)
    )
    group_n2, normed2_t = collect(normed2)
    rows_both, rows_t = (group_n2, group_grad), (normed2_t, cotangent_t)

    send1, keep1, send1b, keep1b, *carry = ffn_call(bits, rows_both, rows_t, big1, True)
    took1, took1b = across(send1, 1), across(send1b, 2)
    grads2, forward, backward, forward_other, backward_other = ffn_call(
        bits, rows_both, rows_t, big2, False, tuple(carry)
    )
    took1, took1b, grads2, forward, backward, forward_other, backward_other = tie(
        took1, took1b, grads2, forward, backward, forward_other, backward_other
    )
    grads2 = lax.psum_scatter(grads2, "dp", scatter_dimension=0)
    backward_other = exchange(backward_other)
    first1, second1 = narrow(add_wide(keep1, took1)), narrow(add_wide(keep1b, took1b))
    y_bit, x_bit = place_bits()[1:]
    keep1, keep1b = pick(first1, y_bit), pick(second1, x_bit)
    took1, took1b = across(pick(first1, 1 - y_bit), 2), across(pick(second1, 1 - x_bit), 1)
    grad_middle, narrowed, gain_two_grad = row_call(
        middle_back_kernel,
        "middle_back",
        (backward, backward_other, middle, gain2, out_grad),
        (wide_rows, narrow_rows, gain_row),
    )
    group_gm, grads_t = collect(narrowed)
    s_send, s_keep, s_sendb, s_keepb, own, other, kernel_grad = mixer_back_call(
        bits, group_gm, grads_t, normed1_t, conv_kernel, saved, mixer_weights
    )
    took1, took1b, s_send, s_keep, s_sendb, s_keepb, own, other, kernel_grad = tie(
        took1, took1b, s_send, s_keep, s_sendb, s_keepb, own, other, kernel_grad
    )

    first1, second1 = narrow(add_wide(keep1, took1)), narrow(add_wide(keep1b, took1b))
    s_took, s_tookb = across(s_send, 1), across(s_sendb, 2)
    mine1, theirs1 = reduce_far(jnp.concatenate([first1, second1], -1))
    input_grad, gain_one_grad = row_call(
        input_back_kernel,
        "input_back",
        (own, exchange(other), tokens, gain1, grad_middle),
        (wide_rows, gain_row),
    )
    summed = jnp.concatenate([gain_one_grad, gain_two_grad, kernel_grad.reshape(1, -1)], 1)
    s_took, s_tookb, mine1, theirs1, summed = tie(s_took, s_tookb, mine1, theirs1, summed)
    s_first, s_second = narrow(add_wide(s_keep, s_took)), narrow(add_wide(s_keepb, s_tookb))

    s_first, s_second = reduce_pair(s_first, 2), reduce_pair(s_second, 1)
    mine1 = reduce_middle(mine1, theirs1)
    result = narrow(middle + (forward + exchange(forward_other).astype(jnp.float32)))
    summed = summed + across(summed, 1)
    summed = summed + across(summed, 2)
    s_first, s_second, mine1, summed, result = tie(s_first, s_second, mine1, summed, result)

    grads2, s_first, s_second = tie(grads2, s_first, s_second)
    mine_s, theirs_s = reduce_far(jnp.concatenate([s_first, s_second], 1))
    grads1 = reduce_near(mine1)
    summed = summed + across(summed, 4)
    mine_s, theirs_s, grads1, summed = tie(mine_s, theirs_s, grads1, summed)
    mine_s = reduce_middle(mine_s, theirs_s)
    summed = summed + across(summed, 8)
    mine_s, summed = tie(mine_s, summed)
    small_grads = reduce_near(mine_s)
    gains = summed[0, : 2 * width]
    gains = gains + exchange(gains)
    big_grads = jnp.concatenate([grads1, grads2.astype(jnp.float32)], -1)
    return (
        result,
        input_grad,
        gains[:width],
        jnp.transpose(small_grads[:3], (1, 0, 2)),
        summed[0, 2 * width :].reshape(kernel_grad.shape),
        small_grads[3],
        gains[width:],
        jnp.transpose(big_grads[:2], (1, 0, 2)),
        big_grads[2],
    )


def solution(mesh):
    paired = mesh.shape["dp"] == 16 and mesh.shape["tensor"] == 2
    return jax.shard_map(
        per_device_pairs if paired else per_device,
        mesh=mesh,
        in_specs=(
            P(("dp", "tensor"), None),
            P(),
            P("dp", None, "tensor"),
            P(None, "tensor"),
            P("dp", "tensor"),
            P(),
            P("dp", None, "tensor"),
            P("dp", "tensor"),
            P(("dp", "tensor"), None),
        ),
        out_specs=(
            P(("dp", "tensor"), None),
            P(("dp", "tensor"), None),
            P(),
            P("dp", None, "tensor"),
            P(None, "tensor"),
            P("dp", "tensor"),
            P(),
            P("dp", None, "tensor"),
            P("dp", "tensor"),
        ),
        check_vma=False,
    )
```
